128 devices in a mesh: gossip: 8 (over z_lo, y), shard: 16 (over x, z_hi, core).
Axes of the slice: x: 4, y: 4, z: 4 (z_hi: 2, z_lo: 2; z = z_hi * 2 + z_lo), core: 2. Of those that a mesh axis runs over, the one named last changes fastest.
Arguments:
- images: bfloat16 [8, 128, 7, 7, 1024], P('gossip', 'shard'), may hold values from -6 to 6
- cotangent: bfloat16 [8, 128, 7, 7, 1024], P('gossip', 'shard'), may hold values from -2 to 2
- weight_in: float32 [8, 1024, 4096], P('gossip', 'shard'), may hold values from -0.1875 to 0.1875
- weight_out: float32 [8, 4096, 1024], P('gossip', 'shard'), may hold values from -0.09375 to 0.09375
- channel_table: float32 [8, 1024, 54], P('gossip', 'shard'), may hold values from -0.6 to 1.4, as said below
- bias_in: float32 [8, 4096], P('gossip', 'shard'), may hold values from -3 to 3
- moment_in: float32 [8, 1024, 4096], P('gossip', 'shard'), may hold values from -6 to 6
- moment_out: float32 [8, 4096, 1024], P('gossip', 'shard'), may hold values from -6 to 6
- moment_table: float32 [8, 1024, 54], P('gossip', 'shard'), may hold values from -6 to 6
- moment_bias: float32 [8, 4096], P('gossip', 'shard'), may hold values from -6 to 6
- step_index: int32 [1], replicated, may hold values from 0 to 2999
Outputs:
- new_weight_in: float32 [8, 1024, 4096], P('gossip', 'shard')
- new_weight_out: float32 [8, 4096, 1024], P('gossip', 'shard')
- new_table: float32 [8, 1024, 54], P('gossip', 'shard')
- new_bias_in: float32 [8, 4096], P('gossip', 'shard')
- new_moment_in: float32 [8, 1024, 4096], P('gossip', 'shard')
- new_moment_out: float32 [8, 4096, 1024], P('gossip', 'shard')
- new_moment_table: float32 [8, 1024, 54], P('gossip', 'shard')
- new_moment_bias: float32 [8, 4096], P('gossip', 'shard')
The draws below stay inside these ranges and needn't reach their ends.
Inputs may be any that keep to these rules, and one draw needn't show every extreme that they name: `channel_table`: per-channel parameters of order one; taps near 1/7 in size, gains and layer scales positive.
All inputs are finite; a program needn't handle non-finite values.
Results may differ from the reference program's by a relative error of at most 0.02.
Values may be sent and summed in bfloat16 or wider, within the bound.
No kernel may reach another device: no remote copies, remote signals or barrier semaphores. Data moves between devices by JAX's collectives and lax.ppermute only.
A program may use at most 128 MiB of HBM per device.

```python
import jax
import jax.numpy as jnp
from jax import lax

CHANNELS = 1024
INNER = 4096
SIDE = 7
IMAGES = 128
N_GOSSIP = 8
N_SHARD = 16


def draw_channel_table(key, part):
    key = jax.random.fold_in(key, 11)
    keys = jax.random.split(key, 6)
    taps = jax.random.truncated_normal(keys[0], -3.0, 3.0, (N_GOSSIP, CHANNELS, 49), jnp.float32) / 7.0
    dw_bias = 0.2 * jax.random.truncated_normal(keys[1], -3.0, 3.0, (N_GOSSIP, CHANNELS, 1), jnp.float32)
    gains = jax.random.uniform(keys[2], (N_GOSSIP, CHANNELS, 1), jnp.float32, 0.6, 1.4)
    shifts = 0.2 * jax.random.truncated_normal(keys[3], -3.0, 3.0, (N_GOSSIP, CHANNELS, 1), jnp.float32)
    out_bias = 0.2 * jax.random.truncated_normal(keys[4], -3.0, 3.0, (N_GOSSIP, CHANNELS, 1), jnp.float32)
    scales = jax.random.uniform(keys[5], (N_GOSSIP, CHANNELS, 1), jnp.float32, 0.3, 1.0)
    return jnp.concatenate([taps, dw_bias, gains, shifts, out_bias, scales], axis=2)


def strengthened(drawn, stream_key, source, target, blocks, factor):
    owner, partner = [(jnp.arange(drawn.shape[dim]) // (drawn.shape[dim] // blocks)).reshape([-1 if axis == dim else 1 for axis in range(drawn.ndim)]) for dim in (source, target)]
    chosen = jax.random.permutation(stream_key, blocks)[partner]
    strong = (owner == chosen) | (owner == (partner + blocks // 2) % blocks)
    return jnp.where(strong, factor * drawn, drawn)


def level_of(rng, shape, pieces, low, largest):
    def one(axis_at, blocks):
        draws = jax.random.uniform(jax.random.fold_in(jax.random.fold_in(rng, 6), axis_at), (blocks,), jnp.float32, low / len(pieces), largest / len(pieces))
        return jnp.repeat(jnp.exp(draws), shape[axis_at] // blocks).reshape((-1,) + (1,) * (len(shape) - axis_at - 1))

    loudness = one(*pieces[0])
    for cut in pieces[1:]:
        loudness = loudness * one(*cut)
    return loudness


def noise(own_key, extent, deviation, limit, shards=(), kind=jnp.bfloat16):
    drawn = deviation * jax.random.normal(own_key, extent, jnp.float32)
    if shards:
        drawn = drawn * level_of(own_key, extent, shards, -0.22, 0.18)
    return jnp.clip(drawn, -limit, limit).astype(kind)


def bell_draw_with(own_key, dims, spread, reach, cuts, heavy, kind=jnp.bfloat16):
    entries = spread * jax.random.normal(own_key, dims, jnp.float32)
    if cuts:
        entries = entries * level_of(own_key, dims, cuts, -0.22, 0.18)
    return jnp.clip(strengthened(entries, jax.random.fold_in(own_key, 3), *heavy), -reach, reach).astype(kind)


def setup_inputs(seed: int = 0) -> dict:
    streams_of = jax.random.split(jax.random.key(seed), 12)
    images = noise(streams_of[0], (N_GOSSIP, IMAGES, SIDE, SIDE, CHANNELS), 1.0, 6.0, ((0, 8), (1, 16)))
    cotangent = bell_draw_with(streams_of[1], (N_GOSSIP, IMAGES, SIDE, SIDE, CHANNELS), 0.1, 2.0, ((0, 8), (1, 16)), (1, 4, 16, 2.0))
    weight_in = noise(streams_of[2], (N_GOSSIP, CHANNELS, INNER), CHANNELS ** -0.5, 0.1875, ((0, 8), (1, 16)), jnp.float32)
    weight_out = noise(streams_of[3], (N_GOSSIP, INNER, CHANNELS), INNER ** -0.5, 0.09375, ((0, 8), (1, 16)), jnp.float32)
    channel_table = draw_channel_table(jax.random.fold_in(streams_of[11], 71), 0)
    bias_in = noise(streams_of[5], (N_GOSSIP, INNER), 0.2, 3.0, ((0, 8), (1, 16)), jnp.float32)
    moment_in = noise(streams_of[6], (N_GOSSIP, CHANNELS, INNER), 1.0, 6.0, ((0, 8), (1, 16)), jnp.float32)
    moment_out = noise(streams_of[7], (N_GOSSIP, INNER, CHANNELS), 1.0, 6.0, ((0, 8), (1, 16)), jnp.float32)
    moment_table = noise(streams_of[8], (N_GOSSIP, CHANNELS, 54), 0.5, 6.0, ((0, 8), (1, 16)), jnp.float32)
    moment_bias = noise(streams_of[9], (N_GOSSIP, INNER), 1.0, 6.0, ((0, 8), (1, 16)), jnp.float32)
    step_index = jax.random.randint(streams_of[10], (1,), 0, 3000).astype(jnp.int32)
    return dict(images=images, cotangent=cotangent, weight_in=weight_in, weight_out=weight_out, channel_table=channel_table, bias_in=bias_in, moment_in=moment_in, moment_out=moment_out, moment_table=moment_table, moment_bias=moment_bias, step_index=step_index)


EPSILON = 1e-06
LEARN_RATE = 0.01
MOMENTUM_BETA = 0.9

def transpose_dot(left, right):
    return lax.dot_general(left, right, (((0,), (0,)), ((), ())), preferred_element_type=jnp.float32)

def back_dot(left, right):
    return lax.dot_general(left, right, (((1,), (1,)), ((), ())), preferred_element_type=jnp.float32)

def gelu_slope(pre_act):
    return 0.5 * (1.0 + lax.erf(pre_act * 0.7071067811865476)) + pre_act * jnp.exp(-0.5 * pre_act * pre_act) * 0.3989422804014327

def forward_pass(images, weight_in, weight_out, channel_table, bias_in):
    side = images.shape[1]
    width = images.shape[3]
    table_float = channel_table.astype(jnp.float32)
    kernel = table_float[:, :49].T.reshape(7, 7, width)
    padded = jnp.pad(images.astype(jnp.float32), ((0, 0), (3, 3), (3, 3), (0, 0)))
    spatial = jnp.zeros(images.shape, jnp.float32) + table_float[:, 49]
    for shift_row in range(7):
        for shift_col in range(7):
            spatial = spatial + padded[:, shift_row:shift_row + side, shift_col:shift_col + side, :] * kernel[shift_row, shift_col]
    spatial = spatial.reshape(-1, width)
    centred = spatial - lax.optimization_barrier(jnp.mean(spatial, axis=1, keepdims=True))
    inverse = lax.rsqrt(lax.optimization_barrier(jnp.mean(centred * centred, axis=1, keepdims=True)) + EPSILON)
    normed = centred * inverse
    normal_out = (normed * table_float[:, 50] + table_float[:, 51]).astype(jnp.bfloat16)
    pre_act = jnp.dot(normal_out, weight_in, preferred_element_type=jnp.float32) + bias_in.astype(jnp.float32)
    activ = jax.nn.gelu(pre_act, approximate=False).astype(jnp.bfloat16)
    branch = jnp.dot(activ, weight_out, preferred_element_type=jnp.float32) + table_float[:, 52]
    return (padded, inverse, normed, normal_out, pre_act, activ, branch)

def pointwise_back(state, cotangent, weight_in, weight_out, channel_table):
    padded, inverse, normed, normal_out, pre_act, activ, branch = state
    width = branch.shape[1]
    table_float = channel_table.astype(jnp.float32)
    upstream = cotangent.reshape(-1, width).astype(jnp.float32)
    grad_scale = lax.optimization_barrier(jnp.sum(upstream * branch, axis=0))
    grad_branch = upstream * table_float[:, 53]
    grad_bias_out = lax.optimization_barrier(jnp.sum(grad_branch, axis=0))
    branch_low = grad_branch.astype(jnp.bfloat16)
    grad_weight_out = transpose_dot(activ, branch_low)
    grad_activ = back_dot(branch_low, weight_out)
    grad_pre = grad_activ * gelu_slope(pre_act)
    grad_bias_in = lax.optimization_barrier(jnp.sum(grad_pre, axis=0))
    pre_low = grad_pre.astype(jnp.bfloat16)
    grad_weight_in = transpose_dot(normal_out, pre_low)
    grad_normal = back_dot(pre_low, weight_in)
    return (grad_weight_in, grad_weight_out, grad_bias_in, grad_normal, (grad_bias_out, grad_scale))

def channel_back(state, grad_normal, extras, channel_table):
    padded, inverse, normed, normal_out, pre_act, activ, branch = state
    width = branch.shape[1]
    side = padded.shape[1] - 6
    table_float = channel_table.astype(jnp.float32)
    grad_gain = lax.optimization_barrier(jnp.sum(grad_normal * normed, axis=0))
    grad_shift = lax.optimization_barrier(jnp.sum(grad_normal, axis=0))
    scaled = grad_normal * table_float[:, 50]
    grad_spatial = inverse * (scaled - lax.optimization_barrier(jnp.mean(scaled, axis=1, keepdims=True)) - normed * lax.optimization_barrier(jnp.mean(scaled * normed, axis=1, keepdims=True)))
    grad_dw_bias = lax.optimization_barrier(jnp.sum(grad_spatial, axis=0))
    grad_grid = grad_spatial.reshape(padded.shape[0], side, side, width)
    taps = []
    for shift_row in range(7):
        for shift_col in range(7):
            taps.append(lax.optimization_barrier(jnp.sum(padded[:, shift_row:shift_row + side, shift_col:shift_col + side, :] * grad_grid, axis=(0, 1, 2))))
    grad_kernel = jnp.stack(taps, axis=1)
    columns = jnp.stack([grad_dw_bias, grad_gain, grad_shift, extras[0], extras[1]], axis=1)
    return jnp.concatenate([grad_kernel, columns], axis=1)

def reference(images, cotangent, weight_in, weight_out, channel_table, bias_in, moment_in, moment_out, moment_table, moment_bias, step_index):
    per_device = images.shape[1] // N_SHARD

    def group_update(operands):
        group_images = operands[0]
        group_cot = operands[1]
        params = operands[2:6]
        moments = operands[6:10]
        lowered = tuple((p.astype(jnp.bfloat16) for p in params))

        def add_device(totals, device):
            start = (device * per_device).astype(jnp.int32)
            own_images = lax.dynamic_slice_in_dim(group_images, start, per_device, 0)
            own_cot = lax.dynamic_slice_in_dim(group_cot, start, per_device, 0)
            state = forward_pass(own_images, lowered[0], lowered[1], lowered[2], lowered[3])
            grad_in, grad_out, grad_bias, grad_normal, extras = pointwise_back(state, own_cot, lowered[0], lowered[1], lowered[2])
            grad_table = channel_back(state, grad_normal, extras, lowered[2])
            terms = (grad_in, grad_out, grad_table, grad_bias)
            rounded = tuple((lax.optimization_barrier(t.astype(jnp.bfloat16)).astype(jnp.float32) for t in terms))
            return (tuple((a + b for a, b in zip(totals, rounded))), None)
        zeros = tuple((jnp.zeros(p.shape, jnp.float32) for p in params))
        totals = lax.scan(add_device, zeros, jnp.arange(N_SHARD, dtype=jnp.int32))[0]
        new_moments = tuple((MOMENTUM_BETA * m + g for m, g in zip(moments, totals)))
        stepped = tuple((p - LEARN_RATE * m for p, m in zip(params, new_moments)))
        return stepped + new_moments
    results = lax.map(group_update, (images, cotangent, weight_in, weight_out, channel_table, bias_in, moment_in, moment_out, moment_table, moment_bias))
    levels = N_GOSSIP.bit_length() - 1
    distance = jnp.left_shift(jnp.int32(1), (step_index[0] % levels).astype(jnp.int32))
    partner = jnp.bitwise_xor(jnp.arange(N_GOSSIP, dtype=jnp.int32), distance)
    averaged = tuple((0.5 * (r + jnp.take(r, partner, axis=0)) for r in results[:4]))
    return (averaged[0], averaged[1], averaged[2], averaged[3], results[4], results[5], results[6], results[7])
```

```python
from functools import partial

import jax
import jax.numpy as jnp
from jax import lax
from jax.experimental import pallas as pl
from jax.experimental.pallas import tpu as pltpu
from jax.sharding import PartitionSpec as P

EPSILON = 1e-06
LEARN_RATE = 0.01
MOMENTUM_BETA = 0.9
BF = jnp.bfloat16
F32 = jnp.float32
MIB = 1024 * 1024

SPOTS = [(x, t) for x in range(4) for t in range(4)]


def pairs(move):
    out = []
    for x, t in SPOTS:
        to_x, to_t = move(x, t)
        out.append((4 * x + t, 4 * (to_x % 4) + to_t))
    return out


X_UP = pairs(lambda x, t: (x + 1, t))
X_DOWN = pairs(lambda x, t: (x - 1, t))
X_FAR = pairs(lambda x, t: (x + 2, t))
CORE = pairs(lambda x, t: (x, t ^ 1))
DEPTH = pairs(lambda x, t: (x, t ^ 2))
CROSS = pairs(lambda x, t: (x, t ^ 3))


def move(value, route):
    return lax.ppermute(value, "shard", route)


def in_order(t, own, by_core, by_depth, by_cross):
    parts = (own, by_core, by_depth, by_cross)
    out = []
    for a in range(4):
        value = parts[a]
        for mine in (1, 2, 3):
            value = jnp.where(t == mine, parts[a ^ mine], value)
        out.append(value)
    return out


def along_x(x, own, up, down, far):
    parts = (own, up, far, down)
    out = []
    for a in range(4):
        value = parts[a]
        for mine in (1, 2, 3):
            value = jnp.where(x == mine, parts[(a - mine) % 4], value)
        out.append(value)
    return out


def gather_x(own):
    half = own.shape[0] // 2
    down = move(own, X_UP)
    up = move(own, X_DOWN)
    first = move(down[:half], X_UP)
    second = move(up[half:], X_DOWN)
    return own, up, down, jnp.concatenate([first, second], axis=0)


def reduce_x(parts):
    own, up, down, far = parts
    half = own.shape[0] // 2
    first = move(far[:half], X_UP).astype(F32)
    second = move(far[half:], X_DOWN).astype(F32)
    to_up = jnp.concatenate([(up[:half].astype(F32) + first).astype(BF), up[half:]], axis=0)
    to_down = jnp.concatenate([down[:half], (down[half:].astype(F32) + second).astype(BF)], axis=0)
    from_down = move(to_up, X_UP)
    from_up = move(to_down, X_DOWN)
    return own.astype(F32) + from_down.astype(F32) + from_up.astype(F32)


def vmem(count):
    return [pl.BlockSpec(memory_space=pltpu.VMEM)] * count


def smem():
    return pl.BlockSpec(memory_space=pltpu.SMEM)


def call(body, ins, outs, scratch=(), flops=0, moved=0, limit=48):
    return pl.pallas_call(
        body,
        out_shape=[jax.ShapeDtypeStruct(shape, kind) for shape, kind in outs],
        in_specs=[smem()] + vmem(ins),
        out_specs=vmem(len(outs)),
        scratch_shapes=list(scratch),
        compiler_params=pltpu.CompilerParams(vmem_limit_bytes=limit * MIB),
        cost_estimate=pl.CostEstimate(flops=flops, bytes_accessed=moved, transcendentals=0),
    )


def cut_body(spot, win, wout, *outs):
    for r in range(4):
        for block in range(4):
            start = pl.multiple_of((4 * block + spot[4 + r]) * 256, 256)
            outs[r][:, 256 * block : 256 * block + 256] = win[:, pl.ds(start, 256)].astype(BF)
    outs[4][...] = wout[...].astype(BF)


def cut(spot, win, wout):
    return call(
        cut_body,
        2,
        [((64, 1024), BF)] * 4 + [((256, 1024), BF)],
        flops=1000000,
        moved=3 * MIB,
    )(spot, win, wout)


def spans(rows):
    return [(start, min(112, rows - start)) for start in range(0, rows, 112)]


def norm_body(spot, images, table, normal_out, normed, inverse, wide, spatial):
    wide[...] = images[...].astype(F32)

    def lanes_step(block, carry):
        lanes = pl.ds(pl.multiple_of(block * 128, 128), 128)
        for i in range(7):
            acc = [jnp.broadcast_to(table[49:50, lanes], (8, 128)) for _ in range(7)]
            for r in range(7):
                row = i + r - 3
                if row < 0 or row > 6:
                    continue
                taps = [jnp.broadcast_to(table[7 * r + q : 7 * r + q + 1, lanes], (8, 128)) for q in range(7)]
                line = [wide[7 * row + j, :, lanes] for j in range(7)]
                for j in range(7):
                    for q in range(7):
                        if 0 <= j + q - 3 <= 6:
                            acc[j] = acc[j] + line[j + q - 3] * taps[q]
            for j in range(7):
                at = 8 * (7 * i + j)
                spatial[at : at + 8, lanes] = acc[j]
        return carry

    lax.fori_loop(0, 8, lanes_step, 0)
    gain = table[50:51, :]
    shift = table[51:52, :]
    for start, size in spans(392):
        rows = slice(start, start + size)
        value = spatial[rows, :]
        centred = value - jnp.mean(value, axis=1, keepdims=True)
        scale = lax.rsqrt(jnp.mean(centred * centred, axis=1, keepdims=True) + EPSILON)
        unit = centred * scale
        shaped = (unit * gain + shift).astype(BF)
        inverse[rows, :] = jnp.broadcast_to(scale, (size, 128))
        for block in range(4):
            normed[block, rows, :] = unit[:, 256 * block : 256 * block + 256]
            normal_out[block, rows, :] = shaped[:, 256 * block : 256 * block + 256]


def norm(spot, images, table):
    return call(
        norm_body,
        2,
        [((4, 392, 256), BF), ((4, 392, 256), F32), ((392, 128), F32)],
        [pltpu.VMEM((49, 8, 1024), F32), pltpu.VMEM((392, 1024), F32)],
        flops=40000000,
        moved=4 * MIB,
    )(spot, images, table)


def normal_parts(value):
    bell = jnp.exp(-0.5 * value * value)
    t = 1.0 / (1.0 + (0.3275911 * 0.7071067811865476) * jnp.abs(value))
    poly = t * (
        0.5 * 0.254829592
        + t * (0.5 * -0.284496736 + t * (0.5 * 1.421413741 + t * (0.5 * -1.453152027 + t * (0.5 * 1.061405429))))
    )
    tail = poly * bell
    return jnp.where(value < 0.0, tail, 1.0 - tail), bell


def dot(left, right, left_dim, right_dim):
    return lax.dot_general(left, right, (((left_dim,), (right_dim,)), ((), ())), preferred_element_type=F32)


def ahead_body(spot, *refs):
    normal = refs[0:4]
    cot = refs[4:8]
    win = refs[8:12]
    wout = refs[12:16]
    table = refs[16]
    slope = refs[17]
    grads = refs[18:22]
    extras = refs[22]
    activ = refs[23]

    def block_step(block, carry):
        lanes = pl.ds(pl.multiple_of(block * 256, 256), 256)
        bias = table[54:55, lanes]
        for r in range(4):
            pre = dot(normal[r][spot[0]], win[0][:, lanes], 1, 0)
            for k in range(1, 4):
                pre = pre + dot(normal[r][spot[k]], win[k][:, lanes], 1, 0)
            pre = pre + bias
            phi, bell = normal_parts(pre)
            activ[r, block] = (pre * phi).astype(BF)
            slope[r, block] = (phi + pre * bell * 0.3989422804014327).astype(BF)
        return carry

    lax.fori_loop(0, 4, block_step, 0)
    scale = table[53:54, :]
    grad_scale = jnp.sum(cot[0][...].astype(F32), axis=0, keepdims=True)
    extras[0:1, :] = grad_scale * scale
    grad_scale = grad_scale * table[52:53, :]
    for k in (3, 1, 2, 0):
        total = dot(activ[0, spot[k]], cot[0][...], 0, 0)
        for r in range(1, 4):
            total = total + dot(activ[r, spot[k]], cot[r][...], 0, 0)
        grad_scale = grad_scale + jnp.sum(total * wout[k][...].astype(F32), axis=0, keepdims=True)
        grads[k][...] = (total * scale).astype(BF)
    extras[1:2, :] = grad_scale


def ahead(spot, normal, cot, win, wout, table):
    out = call(
        ahead_body,
        17,
        [((4, 4, 392, 256), BF)] + [((256, 1024), BF)] * 4 + [((2, 1024), F32)],
        [pltpu.VMEM((4, 4, 392, 256), BF)],
        flops=4 * 1568 * 1024 * 1024,
        moved=16 * MIB,
    )(spot, *normal, *cot, *win, *wout, table)
    return out[0], out[1:5], out[5]


def back_body(spot, *refs):
    cot = refs[0:4]
    slope = refs[4]
    win = refs[5:9]
    wout = refs[9:13]
    table = refs[13]
    pre_low = refs[14]
    grad_normal = refs[15:19]
    bias = refs[19]
    low = refs[20]
    scale = table[53:54, :]
    for r in range(4):
        low[r] = (cot[r][...].astype(F32) * scale).astype(BF)
    for k in range(4):
        total = jnp.zeros((1, 256), F32)
        for r in range(4):
            grad = dot(low[r], wout[k][...], 1, 1) * slope[r, spot[k]].astype(F32)
            total = total + jnp.sum(grad, axis=0, keepdims=True)
            pre_low[r, spot[k]] = grad.astype(BF)
        bias[spot[k]] = total
    for k in range(4):
        for r in range(4):
            grad = dot(pre_low[r, 0], win[k][:, 0:256], 1, 1)
            for block in range(1, 4):
                grad = grad + dot(pre_low[r, block], win[k][:, 256 * block : 256 * block + 256], 1, 1)
            grad_normal[r][spot[k]] = grad.astype(grad_normal[r].dtype)


def back(spot, cot, slope, win, wout, table):
    slab = (4, 392, 256)
    out = call(
        back_body,
        14,
        [((4,) + slab, BF), (slab, F32), (slab, BF), (slab, F32), (slab, BF), ((4, 1, 256), F32)],
        [pltpu.VMEM((4, 392, 1024), BF)],
        flops=4 * 1568 * 1024 * 1024,
        moved=18 * MIB,
    )(spot, *cot, slope, *win, *wout, table)
    return out[0], out[1:5], out[5]


def weight_body(spot, *refs):
    normal = refs[0:4]
    pre_low = refs[4]
    grads = refs[5:9]
    for k in (3, 1, 2, 0):
        for block in range(4):
            total = dot(normal[0][spot[k]], pre_low[0, block], 0, 0)
            for r in range(1, 4):
                total = total + dot(normal[r][spot[k]], pre_low[r, block], 0, 0)
            grads[k][:, 256 * block : 256 * block + 256] = total.astype(BF)


def weight(spot, normal, pre_low):
    return call(
        weight_body,
        5,
        [((256, 1024), BF)] * 4,
        flops=2 * 1568 * 1024 * 1024,
        moved=8 * MIB,
    )(spot, *normal, pre_low)


def channel_body(spot, images, own, by_core, by_depth, normed, inverse, table, bias, extras, out, wide, grid):
    wide[...] = images[...].astype(F32)
    gain_sum = [jnp.zeros((1, 256), F32) for _ in range(4)]
    shift_sum = [jnp.zeros((1, 256), F32) for _ in range(4)]
    dw_sum = [jnp.zeros((1, 256), F32) for _ in range(4)]
    for start, size in spans(392):
        rows = slice(start, start + size)
        grads = []
        mean = jnp.zeros((size, 1), F32)
        cross = jnp.zeros((size, 1), F32)
        for block in range(4):
            cols = slice(256 * block, 256 * block + 256)
            grad = own[block, rows, :] + by_core[block, rows, :].astype(F32) + by_depth[block, rows, :].astype(F32)
            unit = normed[block, rows, :]
            gain_sum[block] += jnp.sum(grad * unit, axis=0, keepdims=True)
            shift_sum[block] += jnp.sum(grad, axis=0, keepdims=True)
            scaled = grad * table[50:51, cols]
            mean += jnp.sum(scaled, axis=1, keepdims=True)
            cross += jnp.sum(scaled * unit, axis=1, keepdims=True)
            grads.append(scaled)
        mean = mean * (1.0 / 1024.0)
        cross = cross * (1.0 / 1024.0)
        factor = inverse[rows, 0:1]
        for block in range(4):
            cols = slice(256 * block, 256 * block + 256)
            value = factor * (grads[block] - mean - normed[block, rows, :] * cross)
            dw_sum[block] += jnp.sum(value, axis=0, keepdims=True)
            grid[rows, cols] = value
    for block in range(4):
        cols = slice(256 * block, 256 * block + 256)
        out[block, 49:50, :] = dw_sum[block]
        out[block, 50:51, :] = gain_sum[block]
        out[block, 51:52, :] = shift_sum[block]
        out[block, 52:54, :] = extras[:, cols]
        out[block, 54:55, :] = bias[block]
        out[block, 55:56, :] = jnp.zeros((1, 256), F32)

    def lanes_step(block, carry):
        lanes = pl.ds(pl.multiple_of(block * 128, 128), 128)
        to_lanes = pl.ds(pl.multiple_of((block % 2) * 128, 128), 128)
        for r in range(7):
            acc = [jnp.zeros((8, 128), F32) for _ in range(7)]
            for i in range(7):
                row = i + r - 3
                if row < 0 or row > 6:
                    continue
                line = [wide[7 * row + j, :, lanes] for j in range(7)]
                grads = [grid[8 * (7 * i + j) : 8 * (7 * i + j) + 8, lanes] for j in range(7)]
                for q in range(7):
                    for j in range(7):
                        if 0 <= j + q - 3 <= 6:
                            acc[q] = acc[q] + line[j + q - 3] * grads[j]
            for q in range(7):
                out[block // 2, 7 * r + q : 7 * r + q + 1, to_lanes] = jnp.sum(acc[q], axis=0, keepdims=True)
        return carry

    lax.fori_loop(0, 8, lanes_step, 0)


def channel(spot, images, own, by_core, by_depth, normed, inverse, table, bias, extras):
    return call(
        channel_body,
        9,
        [((4, 56, 256), F32)],
        [pltpu.VMEM((49, 8, 1024), F32), pltpu.VMEM((392, 1024), F32)],
        flops=60000000,
        moved=7 * MIB,
    )(spot, images, own, by_core, by_depth, normed, inverse, table, bias, extras)[0]


def step_body(spot, own, by_core, by_depth, by_cross, param, moment, new_moment, stepped, low):
    pieces = (own, by_core, by_depth, by_cross)
    for r in range(4):
        for block in range(4):
            lanes = pl.ds(pl.multiple_of((4 * block + spot[4 + r]) * 256, 256), 256)
            grad = pieces[r][:, 256 * block : 256 * block + 256].astype(F32)
            fresh = MOMENTUM_BETA * moment[:, lanes] + grad
            after = param[:, lanes] - LEARN_RATE * fresh
            new_moment[:, lanes] = fresh
            stepped[:, lanes] = after
            low[:, lanes] = after.astype(BF)


def step(spot, pieces, param, moment):
    return call(
        step_body,
        6,
        [((64, 4096), F32), ((64, 4096), F32), ((64, 4096), BF)],
        flops=1000000,
        moved=6 * MIB,
    )(spot, *pieces, param, moment)


def run(
    level,
    images,
    cotangent,
    weight_in,
    weight_out,
    channel_table,
    bias_in,
    moment_in,
    moment_out,
    moment_table,
    moment_bias,
):
    place = lax.axis_index("shard")
    x = place // 4
    t = place % 4
    spot = jnp.stack([x, (x + 1) % 4, (x + 3) % 4, (x + 2) % 4, t, t ^ 1, t ^ 2, t ^ 3]).astype(jnp.int32)
    grid_images = images[0].transpose(1, 2, 0, 3).reshape(49, 8, 1024)
    grid_cot = cotangent[0].transpose(1, 2, 0, 3).reshape(392, 1024)

    table_own = channel_table[0].T
    table_low = table_own.astype(BF)
    quarter = in_order(t, table_low, move(table_low, CORE), move(table_low, DEPTH), move(table_low, CROSS))
    bias_low = bias_in.astype(BF)
    packed = jnp.concatenate([jnp.concatenate(quarter, axis=1), bias_low, jnp.zeros_like(bias_low)], axis=0)
    packed_down = move(packed, X_UP)
    packed_up = move(packed, X_DOWN)
    packed_far = move(packed, X_FAR)
    table = jnp.concatenate(along_x(x, packed, packed_up, packed_down, packed_far), axis=1).astype(F32)

    cuts = cut(spot, weight_in[0], weight_out[0])
    rows = in_order(t, cuts[0], move(cuts[1], CORE), move(cuts[2], DEPTH), move(cuts[3], CROSS))
    win = gather_x(jnp.concatenate(rows, axis=0))
    wout = gather_x(cuts[4])

    normal_out, normed, inverse = norm(spot, grid_images, table)
    normal_depth = move(normal_out, DEPTH)
    normal = (normal_out, move(normal_out, CORE), normal_depth, move(normal_depth, CORE))
    cot_depth = move(grid_cot, DEPTH)
    cot = (grid_cot, move(grid_cot, CORE), cot_depth, move(cot_depth, CORE))

    slope, grads_out, extras = ahead(spot, normal, cot, win, wout, table)
    total_out = reduce_x(grads_out)
    pre_low, grad_normal, grad_bias = back(spot, cot, slope, win, wout, table)
    grads_in = weight(spot, normal, pre_low)
    total_in = reduce_x(grads_in)

    by_core = move(grad_normal[1], CORE)
    also = move(grad_normal[3], CORE)
    by_depth = move((grad_normal[2] + also.astype(F32)).astype(BF), DEPTH)
    small = channel(
        spot, grid_images, grad_normal[0], by_core, by_depth, normed, inverse, table, grad_bias, extras
    )

    def pick(index):
        return lax.dynamic_index_in_dim(small, index, 0, keepdims=False)

    small_sum = (
        pick(x)
        + move(pick(spot[1]).astype(BF), X_UP).astype(F32)
        + move(pick(spot[2]).astype(BF), X_DOWN).astype(F32)
        + move(pick(spot[3]).astype(BF), X_FAR).astype(F32)
    )
    by_t = in_order(t, *[small_sum[:54, 64 * a : 64 * a + 64] for a in range(4)])
    total_table = (
        by_t[0]
        + move(by_t[1].astype(BF), CORE).astype(F32)
        + move(by_t[2].astype(BF), DEPTH).astype(F32)
        + move(by_t[3].astype(BF), CROSS).astype(F32)
    )
    total_bias = small_sum[54:55, :]

    def rows_of(index):
        return lax.dynamic_slice_in_dim(total_in, 64 * index, 64, 0).astype(BF)

    pieces = (
        rows_of(spot[4]),
        move(rows_of(spot[5]), CORE),
        move(rows_of(spot[6]), DEPTH),
        move(rows_of(spot[7]), CROSS),
    )
    new_moment_in, stepped_in, low_in = step(spot, pieces, weight_in[0], moment_in[0])

    def update(param, moment, grad):
        fresh = MOMENTUM_BETA * moment + grad
        return fresh, param - LEARN_RATE * fresh

    new_moment_out, stepped_out = update(weight_out[0], moment_out[0], total_out)
    new_moment_table, stepped_table = update(table_own, moment_table[0].T, total_table)
    new_moment_bias, stepped_bias = update(bias_in, moment_bias, total_bias)

    mask = 2**level
    swap = [(g, g ^ mask) for g in range(8)]

    def average(own, low):
        return 0.5 * (own + lax.ppermute(low, "gossip", swap).astype(F32))

    new_out = average(stepped_out, stepped_out.astype(BF))
    new_in = average(stepped_in, low_in)
    stepped_small = jnp.concatenate([stepped_table, stepped_bias.reshape(4, 64)], axis=0)
    new_small = average(stepped_small, stepped_small.astype(BF))
    return (
        new_in[None],
        new_out[None],
        new_small[:54].T[None],
        new_small[54:].reshape(1, 256),
        new_moment_in[None],
        new_moment_out[None],
        new_moment_table.T[None],
        new_moment_bias,
    )


def on_device(*args):
    levels = lax.axis_size("gossip").bit_length() - 1
    return lax.switch(args[-1][0] % levels, [partial(run, level) for level in range(levels)], *args[:-1])


def solution(mesh):
    in_specs = (
        P("gossip", "shard", None, None, None),
        P("gossip", "shard", None, None, None),
        P("gossip", "shard", None),
        P("gossip", "shard", None),
        P("gossip", "shard", None),
        P("gossip", "shard"),
        P("gossip", "shard", None),
        P("gossip", "shard", None),
        P("gossip", "shard", None),
        P("gossip", "shard"),
        P(),
    )
    out_specs = (
        P("gossip", "shard", None),
        P("gossip", "shard", None),
        P("gossip", "shard", None),
        P("gossip", "shard"),
        P("gossip", "shard", None),
        P("gossip", "shard", None),
        P("gossip", "shard", None),
        P("gossip", "shard"),
    )
    return jax.shard_map(
        on_device, mesh=mesh, in_specs=in_specs, out_specs=out_specs, check_vma=False
    )
```

```python
from functools import partial

import jax
import jax.numpy as jnp
from jax import lax
from jax.experimental import pallas as pl
from jax.experimental.pallas import tpu as pltpu
from jax.sharding import PartitionSpec as P

EPSILON = 1e-06
LEARN_RATE = 0.01
MOMENTUM_BETA = 0.9
BF = jnp.bfloat16
F32 = jnp.float32
MIB = 1024 * 1024

SPOTS = [(x, t) for x in range(4) for t in range(4)]


def pairs(move):
    out = []
    for x, t in SPOTS:
        to_x, to_t = move(x, t)
        out.append((4 * x + t, 4 * (to_x % 4) + to_t))
    return out


X_UP = pairs(lambda x, t: (x + 1, t))
X_DOWN = pairs(lambda x, t: (x - 1, t))
X_FAR = pairs(lambda x, t: (x + 2, t))
X_NEXT = pairs(lambda x, t: (x ^ 1, t))
CORE = pairs(lambda x, t: (x, t ^ 1))
DEPTH = pairs(lambda x, t: (x, t ^ 2))
CROSS = pairs(lambda x, t: (x, t ^ 3))


def move(value, route):
    return lax.ppermute(value, "shard", route)


def in_order(t, pieces):
    out = []
    for a in range(4):
        value = pieces[a]
        for mine in (1, 2, 3):
            value = jnp.where(t == mine, pieces[a ^ mine], value)
        out.append(value)
    return out


def vmem(count):
    return [pl.BlockSpec(memory_space=pltpu.VMEM)] * count


def smem():
    return pl.BlockSpec(memory_space=pltpu.SMEM)


def after(value, *first):
    return lax.optimization_barrier((value,) + first)[0]


def call(body, ins, outs, scratch=(), limit=16, micros=1):
    return pl.pallas_call(
        body,
        out_shape=[jax.ShapeDtypeStruct(shape, kind) for shape, kind in outs],
        in_specs=[smem()] + vmem(ins),
        out_specs=vmem(len(outs)),
        scratch_shapes=list(scratch),
        compiler_params=pltpu.CompilerParams(vmem_limit_bytes=limit * MIB),
        cost_estimate=pl.CostEstimate(flops=micros * 1000000000, bytes_accessed=1000, transcendentals=0),
    )


def cut_body(spot, win, wout, table, *outs):
    for r in range(4):
        piece = outs[min(r, 2)]
        base = 80 if r == 3 else 0
        for block in range(4):
            start = pl.multiple_of((4 * block + spot[4 + r]) * 256, 256)
            piece[base : base + 64, 256 * block : 256 * block + 256] = win[:, pl.ds(start, 256)].astype(BF)
        for g in range(4):
            size = min(16, 54 - 16 * g)
            rows = table[16 * g : 16 * g + size, :]
            if size < 16:
                rows = jnp.concatenate([rows, jnp.zeros((8 - size, 64), F32), jnp.zeros((8, 64), F32)], axis=0)
            wide = jnp.concatenate([rows, jnp.zeros((16, 64), F32)], axis=1)
            piece[base + 64 : base + 80, 128 * g : 128 * g + 128] = wide.astype(BF)
        piece[base + 64 : base + 80, 512:1024] = jnp.zeros((16, 512), BF)
    outs[3][...] = wout[...].astype(BF)


def cut(spot, win, wout, table):
    return call(cut_body, 3, [((80, 1024), BF)] * 2 + [((160, 1024), BF), ((256, 1024), BF)])(spot, win, wout, table)


def join_body(spot, own, by_depth, both, bias, joined, tail):
    pieces = (own, both.at[0:80], by_depth.at[0:80], both.at[80:160])
    for r in range(4):
        joined[pl.ds(pl.multiple_of(64 * spot[4 + r], 64), 64), :] = pieces[r][0:64, :]
    for g in range(4):
        parts = [pieces[r][64:80, 128 * g : 128 * g + 64].astype(F32) for r in range(4)]
        for a in range(4):
            value = parts[0]
            for r in (1, 2, 3):
                value = jnp.where(spot[4 + r] == a, parts[r], value)
            tail[:, 256 * g + 64 * a : 256 * g + 64 * a + 64] = value
    tail[6:7, 768:1024] = bias[...]
    joined[256:272, :] = tail[...].astype(BF)


def join(spot, own, by_depth, both, bias):
    return call(join_body, 4, [((272, 1024), BF)], [pltpu.VMEM((16, 1024), F32)])(spot, own, by_depth, both, bias)[0]


def spans(rows):
    return [(start, min(112, rows - start)) for start in range(0, rows, 112)]


def norm_body(spot, own, near, *refs):
    packs = refs[0:4]
    normal_out, normed, inverse, table, wide, spatial = refs[4:]
    for k in range(4):
        lanes = pl.ds(pl.multiple_of(256 * spot[k], 256), 256)
        for g in range(4):
            table[16 * g : 16 * g + 16, lanes] = packs[k][:, 256 * g : 256 * g + 256].astype(F32)
    wide[0] = own[...].astype(F32)
    wide[1] = near[...].astype(F32)

    def lanes_step(at, carry):
        block = at % 8
        part = at // 8
        lanes = pl.ds(pl.multiple_of(block * 128, 128), 128)
        for i in range(7):
            acc = [jnp.broadcast_to(table[49:50, lanes], (8, 128)) for _ in range(7)]
            for r in range(7):
                row = i + r - 3
                if row < 0 or row > 6:
                    continue
                taps = [jnp.broadcast_to(table[7 * r + q : 7 * r + q + 1, lanes], (8, 128)) for q in range(7)]
                line = [wide[part, 8 * (7 * row + j) : 8 * (7 * row + j) + 8, lanes] for j in range(7)]
                for j in range(7):
                    for q in range(7):
                        if 0 <= j + q - 3 <= 6:
                            acc[j] = acc[j] + line[j + q - 3] * taps[q]
            for j in range(7):
                at_row = 8 * (7 * i + j)
                spatial[part, at_row : at_row + 8, lanes] = acc[j]
        return carry

    lax.fori_loop(0, 16, lanes_step, 0)
    gain = table[50:51, :]
    shift = table[51:52, :]
    for part in range(2):
        for start, size in spans(392):
            rows = slice(start, start + size)
            value = spatial[part, rows, :]
            centred = value - jnp.mean(value, axis=1, keepdims=True)
            scale = lax.rsqrt(jnp.mean(centred * centred, axis=1, keepdims=True) + EPSILON)
            unit = centred * scale
            shaped = (unit * gain + shift).astype(BF)
            inverse[part, rows, :] = jnp.broadcast_to(scale, (size, 128))
            for block in range(4):
                normed[part, block, rows, :] = unit[:, 256 * block : 256 * block + 256]
                normal_out[part, block, rows, :] = shaped[:, 256 * block : 256 * block + 256]


def norm(spot, own, near, packs):
    slabs = (2, 4, 392, 256)
    return call(
        norm_body,
        6,
        [(slabs, BF), (slabs, F32), ((2, 392, 128), F32), ((64, 1024), F32)],
        [pltpu.VMEM((2, 392, 1024), F32), pltpu.VMEM((2, 392, 1024), F32)],
        limit=24,
        micros=9,
    )(spot, own, near, *packs)


def normal_parts(value):
    bell = jnp.exp(-0.5 * value * value)
    t = 1.0 / (1.0 + (0.3275911 * 0.7071067811865476) * jnp.abs(value))
    poly = t * (
        0.5 * 0.254829592
        + t * (0.5 * -0.284496736 + t * (0.5 * 1.421413741 + t * (0.5 * -1.453152027 + t * (0.5 * 1.061405429))))
    )
    tail = poly * bell
    return jnp.where(value < 0.0, tail, 1.0 - tail), bell


def dot(left, right, left_dim, right_dim):
    return lax.dot_general(left, right, (((left_dim,), (right_dim,)), ((), ())), preferred_element_type=F32)


def forward_body(spot, *refs):
    normal = refs[0:2]
    win = refs[2:5] + (refs[10],)
    table = refs[7]
    activ = refs[8]
    slope = refs[9]
    win[3][0:128, :] = refs[5][128:256, :]
    win[3][128:256, :] = refs[6][128:256, :]

    def block_step(block, carry):
        lanes = pl.ds(pl.multiple_of(block * 256, 256), 256)
        bias = table[54:55, lanes]
        for r in range(4):
            pre = dot(normal[r % 2][r // 2, spot[0]], win[0][0:256, lanes], 1, 0)
            for k in range(1, 4):
                pre = pre + dot(normal[r % 2][r // 2, spot[k]], win[k][0:256, lanes], 1, 0)
            pre = pre + bias
            phi, bell = normal_parts(pre)
            activ[r, block] = (pre * phi).astype(BF)
            slope[r, block] = (phi + pre * bell * 0.3989422804014327).astype(BF)
        return carry

    lax.fori_loop(0, 4, block_step, 0)


def forward(spot, normal, win, far, table):
    return call(
        forward_body, 8, [((4, 4, 392, 256), BF)] * 2, [pltpu.VMEM((256, 1024), BF)], limit=24, micros=9
    )(spot, *normal, *win, *far, table)


def outer_body(spot, *refs):
    activ = refs[0]
    cot = refs[1:5]
    wout = refs[5:8]
    far = refs[8:10]
    table = refs[10]
    grads = refs[11:14]
    far_grads = refs[14:16]
    extras = refs[16]
    scale = table[53:54, :]
    grad_scale = jnp.sum(cot[0][...].astype(F32), axis=0, keepdims=True)
    extras[0:1, :] = grad_scale * scale
    grad_scale = grad_scale * table[52:53, :]
    for k in (3, 1, 2, 0):
        total = dot(activ[0, spot[k]], cot[0][...], 0, 0)
        for r in range(1, 4):
            total = total + dot(activ[r, spot[k]], cot[r][...], 0, 0)
        scaled = (total * scale).astype(BF)
        if k == 3:
            for h in range(2):
                rows = slice(128 * h, 128 * h + 128)
                grad_scale = grad_scale + jnp.sum(
                    total[rows] * far[h][0:128, :].astype(F32), axis=0, keepdims=True
                )
                far_grads[h][...] = scaled[rows]
        else:
            grad_scale = grad_scale + jnp.sum(total * wout[k][...].astype(F32), axis=0, keepdims=True)
            grads[k][...] = scaled
    extras[1:2, :] = grad_scale


def outer(spot, activ, cot, wout, far, table):
    out = call(
        outer_body,
        11,
        [((256, 1024), BF)] * 3 + [((128, 1024), BF)] * 2 + [((2, 1024), F32)],
        limit=24,
        micros=6,
    )(spot, activ, *cot, *wout, *far, table)
    return out[0:3], out[3:5], out[5]


def mix_body(spot, up, down, first, second, to_up, to_down):
    to_up[0:128, :] = (up[0:128, :].astype(F32) + first[...].astype(F32)).astype(BF)
    to_up[128:256, :] = up[128:256, :]
    to_down[0:128, :] = down[0:128, :]
    to_down[128:256, :] = (down[128:256, :].astype(F32) + second[...].astype(F32)).astype(BF)


def mix(spot, up, down, first, second):
    return call(mix_body, 4, [((256, 1024), BF)] * 2)(spot, up, down, first, second)


def back_body(spot, *refs):
    cot = refs[0:4]
    slope = refs[4]
    win = refs[5:8] + (refs[18],)
    wout = refs[8:11] + (refs[19],)
    far = refs[11:13]
    table = refs[13]
    pre_low = refs[14]
    home = refs[15]
    away = refs[16]
    bias = refs[17]
    low = refs[20]
    for h in range(2):
        wout[3][128 * h : 128 * h + 128, :] = far[h][0:128, :]
        win[3][128 * h : 128 * h + 128, :] = far[h][128:256, :]
    scale = table[53:54, :]
    for r in range(4):
        low[r] = (cot[r][...].astype(F32) * scale).astype(BF)
    for k in range(4):
        total = jnp.zeros((1, 256), F32)
        for r in range(4):
            grad = dot(low[r], wout[k][...], 1, 1) * slope[r, spot[k]].astype(F32)
            total = total + jnp.sum(grad, axis=0, keepdims=True)
            pre_low[r, spot[k]] = grad.astype(BF)
        bias[spot[k]] = total
    for k in range(4):
        for r in range(4):
            grad = dot(pre_low[r, 0], win[k][0:256, 0:256], 1, 1)
            for block in range(1, 4):
                grad = grad + dot(pre_low[r, block], win[k][0:256, 256 * block : 256 * block + 256], 1, 1)
            if r % 2:
                away[r // 2, spot[k]] = grad.astype(BF)
            else:
                home[r // 2, spot[k]] = grad.astype(BF)


def back(spot, cot, slope, win, wout, far, table):
    return call(
        back_body,
        14,
        [((4, 4, 392, 256), BF), ((2, 4, 392, 256), BF), ((2, 4, 392, 256), BF), ((4, 1, 256), F32)],
        [pltpu.VMEM((256, 1024), BF), pltpu.VMEM((256, 1024), BF), pltpu.VMEM((4, 392, 1024), BF)],
        limit=32,
        micros=10,
    )(spot, *cot, slope, *win, *wout, *far, table)


def weight_body(spot, *refs):
    normal = refs[0:2]
    pre_low = refs[2]
    grads = refs[3:6]
    far_grads = refs[6:8]
    for k in (3, 1, 2, 0):
        for block in range(4):
            cols = slice(256 * block, 256 * block + 256)
            total = dot(normal[0][0, spot[k]], pre_low[0, block], 0, 0)
            for r in range(1, 4):
                total = total + dot(normal[r % 2][r // 2, spot[k]], pre_low[r, block], 0, 0)
            if k == 3:
                for h in range(2):
                    far_grads[h][:, cols] = total[128 * h : 128 * h + 128].astype(BF)
            else:
                grads[k][:, cols] = total.astype(BF)


def weight(spot, normal, pre_low):
    out = call(
        weight_body,
        3,
        [((256, 1024), BF)] * 3 + [((128, 1024), BF)] * 2,
        micros=20,
    )(spot, *normal, pre_low)
    return out[0:3], out[3:5]


def channel_body(spot, images, images_z, home, by_core, normed, inverse, table, bias, extras, *refs):
    outs = refs[0:2]
    out, wide, grid = refs[2:]
    gain_sum = [jnp.zeros((1, 256), F32) for _ in range(4)]
    shift_sum = [jnp.zeros((1, 256), F32) for _ in range(4)]
    dw_sum = [jnp.zeros((1, 256), F32) for _ in range(4)]
    for part, pixels in enumerate((images, images_z)):
        wide[part] = pixels[...].astype(F32)
        for start, size in spans(392):
            rows = slice(start, start + size)
            grads = []
            mean = jnp.zeros((size, 1), F32)
            cross = jnp.zeros((size, 1), F32)
            for block in range(4):
                cols = slice(256 * block, 256 * block + 256)
                grad = home[part, block, rows, :].astype(F32) + by_core[part, block, rows, :].astype(F32)
                unit = normed[part, block, rows, :]
                gain_sum[block] += jnp.sum(grad * unit, axis=0, keepdims=True)
                shift_sum[block] += jnp.sum(grad, axis=0, keepdims=True)
                scaled = grad * table[50:51, cols]
                mean += jnp.sum(scaled, axis=1, keepdims=True)
                cross += jnp.sum(scaled * unit, axis=1, keepdims=True)
                grads.append(scaled)
            mean = mean * (1.0 / 1024.0)
            cross = cross * (1.0 / 1024.0)
            factor = inverse[part, rows, 0:1]
            for block in range(4):
                cols = slice(256 * block, 256 * block + 256)
                value = factor * (grads[block] - mean - normed[part, block, rows, :] * cross)
                dw_sum[block] += jnp.sum(value, axis=0, keepdims=True)
                grid[part, rows, cols] = value
    for block in range(4):
        cols = slice(256 * block, 256 * block + 256)
        out[block, 49:50, :] = dw_sum[block]
        out[block, 50:51, :] = gain_sum[block]
        out[block, 51:52, :] = shift_sum[block]
        out[block, 52:54, :] = extras[:, cols]
        out[block, 54:55, :] = bias[block]
        out[block, 55:56, :] = jnp.zeros((1, 256), F32)

    def lanes_step(block, carry):
        lanes = pl.ds(pl.multiple_of(block * 128, 128), 128)
        to_lanes = pl.ds(pl.multiple_of((block % 2) * 128, 128), 128)
        for r in range(7):
            acc = [jnp.zeros((8, 128), F32) for _ in range(7)]
            for part in range(2):
                for i in range(7):
                    row = i + r - 3
                    if row < 0 or row > 6:
                        continue
                    line = [wide[part, 8 * (7 * row + j) : 8 * (7 * row + j) + 8, lanes] for j in range(7)]
                    grads = [grid[part, 8 * (7 * i + j) : 8 * (7 * i + j) + 8, lanes] for j in range(7)]
                    for q in range(7):
                        for j in range(7):
                            if 0 <= j + q - 3 <= 6:
                                acc[q] = acc[q] + line[j + q - 3] * grads[j]
            for q in range(7):
                out[block // 2, 7 * r + q : 7 * r + q + 1, to_lanes] = jnp.sum(acc[q], axis=0, keepdims=True)
        return carry

    lax.fori_loop(0, 8, lanes_step, 0)
    for h in range(2):
        outs[0][h] = out[spot[8 + h]]
        outs[1][h] = out[spot[10 + h]].astype(BF)


def channel(spot, *operands):
    return call(
        channel_body,
        9,
        [((2, 56, 256), F32), ((2, 56, 256), BF)],
        [pltpu.VMEM((4, 56, 256), F32), pltpu.VMEM((2, 392, 1024), F32), pltpu.VMEM((2, 392, 1024), F32)],
        limit=28,
        micros=2,
    )(spot, *operands)


def rows_body(spot, own, from_down, from_up, *outs):
    for r in range(4):
        rows = pl.ds(pl.multiple_of(64 * spot[4 + r], 64), 64)
        total = own[rows, :].astype(F32) + from_down[rows, :].astype(F32) + from_up[rows, :].astype(F32)
        outs[r // 2][64 * (r % 2) : 64 * (r % 2) + 64, :] = total.astype(BF)


def rows_of(spot, own, from_down, from_up):
    return call(rows_body, 3, [((128, 1024), BF)] * 2)(spot, own, from_down, from_up)


def shift_body(spot, own, from_down, from_up, param, moment, new_moment, stepped, low):
    for start in range(0, 256, 64):
        rows = slice(start, start + 64)
        grad = own[rows, :].astype(F32) + from_down[rows, :].astype(F32) + from_up[rows, :].astype(F32)
        fresh = MOMENTUM_BETA * moment[rows, :] + grad
        moved = param[rows, :] - LEARN_RATE * fresh
        new_moment[rows, :] = fresh
        stepped[rows, :] = moved
        low[rows, :] = moved.astype(BF)


def shift(spot, *operands):
    return call(
        shift_body, 5, [((256, 1024), F32), ((256, 1024), F32), ((256, 1024), BF)], limit=8, micros=6
    )(spot, *operands)


def step_body(spot, *refs):
    here, by_depth, peer_here, peer_depth, by_core = refs[0:5]
    pieces = (here.at[0:64], by_core.at[0:64], by_depth.at[0:64], by_core.at[64:128])
    peers = (peer_here.at[0:64], by_core.at[128:192], peer_depth.at[0:64], by_core.at[192:256])
    param, moment, peer_base, new_param, new_moment = refs[5:]
    for r in range(4):
        for block in range(4):
            lanes = pl.ds(pl.multiple_of((4 * block + spot[4 + r]) * 256, 256), 256)
            cols = slice(256 * block, 256 * block + 256)
            fresh = MOMENTUM_BETA * moment[:, lanes] + pieces[r][:, cols].astype(F32)
            after_step = param[:, lanes] - LEARN_RATE * fresh
            peer = peer_base[:, lanes].astype(F32) - LEARN_RATE * peers[r][:, cols].astype(F32)
            new_moment[:, lanes] = fresh
            new_param[:, lanes] = 0.5 * (after_step + peer)


def step(spot, *operands):
    return call(step_body, 8, [((64, 4096), F32), ((64, 4096), F32)])(spot, *operands)


def run(
    level,
    images,
    cotangent,
    weight_in,
    weight_out,
    channel_table,
    bias_in,
    moment_in,
    moment_out,
    moment_table,
    moment_bias,
):
    place = lax.axis_index("shard")
    x = place // 4
    t = place % 4
    spot = jnp.stack([x, (x + 1) % 4, (x + 3) % 4, (x + 2) % 4, t, t ^ 1, t ^ 2, t ^ 3, x, x ^ 1, x ^ 2, x ^ 3]).astype(jnp.int32)
    grid_images = images[0].transpose(1, 2, 0, 3).reshape(392, 1024)
    grid_cot = cotangent[0].transpose(1, 2, 0, 3).reshape(392, 1024)

    images_z = move(grid_images, DEPTH)
    cot_z = move(after(grid_cot, images_z), DEPTH)

    mask = 2**level
    swap = [(g, g ^ mask) for g in range(8)]

    def partner(value, turn):
        route = [
            (16 * g + 4 * x_at + t_at, 16 * (g ^ mask) + 4 * x_at + (t_at ^ turn))
            for g in range(8)
            for x_at, t_at in SPOTS
        ]
        return lax.ppermute(value, ("gossip", "shard"), route)

    table_own = channel_table[0].T
    cut_own, cut_core, cut_away, wout_own = cut(spot, weight_in[0], weight_out[0], table_own)
    cut_depth = move(cut_away, DEPTH)
    wout_down = move(wout_own, X_UP)
    wout_up = move(wout_own, X_DOWN)
    cut_both = move(jnp.concatenate([cut_core, cut_depth[80:160]], axis=0), CORE)
    joined = join(spot, cut_own, cut_depth, after(cut_both, wout_down, wout_up), bias_in)
    joined_down = move(joined, X_UP)
    joined_up = move(joined, X_DOWN)
    tail_far = move(joined[256:272], X_FAR)
    packs = (joined[256:272], joined_up[256:272], joined_down[256:272], tail_far)
    far = (
        move(jnp.concatenate([wout_down[0:128], joined_down[0:128]], axis=0), X_UP),
        move(jnp.concatenate([wout_up[128:256], joined_up[128:256]], axis=0), X_DOWN),
    )
    win = (joined, joined_up, joined_down)
    wout = (wout_own, wout_up, wout_down)

    normal_own, normed, inverse, table = norm(spot, grid_images, images_z, packs)
    base = weight_in[0] - (LEARN_RATE * MOMENTUM_BETA) * moment_in[0]
    peer_base = partner(after(base.astype(BF), joined), 0)
    normal = (normal_own, move(after(normal_own, *far, peer_base, cot_z), CORE))
    activ, slope = forward(spot, normal, win, far, table)
    cot = (grid_cot, move(after(grid_cot, images_z), CORE), cot_z, move(after(cot_z, normal_own), CORE))
    out_near, out_far, extras = outer(spot, activ, cot, wout, far, table)
    out_first = move(out_far[0], X_UP)
    out_second = move(out_far[1], X_DOWN)
    pre_low, home, away, grad_bias = back(spot, cot, after(slope, extras), win, wout, far, table)
    by_core = move(away, CORE)
    out_up, out_down = mix(spot, after(out_near[1], home), out_near[2], out_first, out_second)
    in_near, in_far = weight(spot, normal, after(pre_low, out_up))

    out_from_down = move(out_up, X_UP)
    out_from_up = move(out_down, X_DOWN)

    small = channel(
        spot,
        grid_images,
        images_z,
        after(home, out_up),
        by_core,
        normed,
        inverse,
        table,
        grad_bias,
        extras,
    )
    in_up, in_down = mix(
        spot, after(in_near[1], small[0]), in_near[2], move(in_far[0], X_UP), move(in_far[1], X_DOWN)
    )
    in_up, in_down, out_from_down, out_from_up = lax.optimization_barrier(
        (in_up, in_down, out_from_down, out_from_up)
    )
    new_moment_out, stepped_out, low_out = shift(
        spot, out_near[0], out_from_down, out_from_up, weight_out[0], moment_out[0]
    )

    def update(param, moment, grad):
        fresh = MOMENTUM_BETA * moment + grad
        return fresh, param - LEARN_RATE * fresh

    in_from_down = move(in_up, X_UP)
    in_from_up = move(in_down, X_DOWN)
    here, away_in = rows_of(spot, after(in_near[0], low_out), in_from_down, in_from_up)

    half_x = small[0] + move(after(small[1], in_from_down), X_FAR).astype(F32)
    small_sum = half_x[0] + move(half_x[1].astype(BF), X_NEXT).astype(F32)
    by_t = in_order(t, [small_sum[:54, 64 * a : 64 * a + 64] for a in range(4)])
    half_t = jnp.stack(by_t[0:2]) + move(jnp.stack(by_t[2:4]).astype(BF), DEPTH).astype(F32)
    total_table = half_t[0] + move(half_t[1].astype(BF), CORE).astype(F32)
    total_bias = small_sum[54:55, :]

    def average(own, low):
        return 0.5 * (own + lax.ppermute(low, "gossip", swap).astype(F32))

    new_out = average(stepped_out, low_out)
    by_depth = move(away_in, DEPTH)
    peer_here = partner(here, 0)
    peer_depth = partner(away_in, 2)
    across = move(
        jnp.concatenate([here[64:128], after(by_depth, new_out)[64:128], peer_here[64:128], peer_depth[64:128]], axis=0), CORE
    )
    new_in, new_moment_in = step(
        spot, here, by_depth, peer_here, peer_depth, across, weight_in[0], moment_in[0], peer_base
    )

    new_moment_table, stepped_table = update(table_own, moment_table[0].T, total_table)
    new_moment_bias, stepped_bias = update(bias_in, moment_bias, total_bias)

    stepped_small = jnp.concatenate([stepped_table, stepped_bias.reshape(4, 64)], axis=0)
    new_small = average(stepped_small, stepped_small.astype(BF))
    return (
        new_in[None],
        new_out[None],
        new_small[:54].T[None],
        new_small[54:].reshape(1, 256),
        new_moment_in[None],
        new_moment_out[None],
        new_moment_table.T[None],
        new_moment_bias,
    )


def on_device(*args):
    levels = lax.axis_size("gossip").bit_length() - 1
    return lax.switch(args[-1][0] % levels, [partial(run, level) for level in range(levels)], *args[:-1])


def solution(mesh):
    in_specs = (
        P("gossip", "shard", None, None, None),
        P("gossip", "shard", None, None, None),
        P("gossip", "shard", None),
        P("gossip", "shard", None),
        P("gossip", "shard", None),
        P("gossip", "shard"),
        P("gossip", "shard", None),
        P("gossip", "shard", None),
        P("gossip", "shard", None),
        P("gossip", "shard"),
        P(),
    )
    out_specs = (
        P("gossip", "shard", None),
        P("gossip", "shard", None),
        P("gossip", "shard", None),
        P("gossip", "shard"),
        P("gossip", "shard", None),
        P("gossip", "shard", None),
        P("gossip", "shard", None),
        P("gossip", "shard"),
    )
    return jax.shard_map(
        on_device, mesh=mesh, in_specs=in_specs, out_specs=out_specs, check_vma=False
    )
```

```python
from functools import partial

import jax
import jax.numpy as jnp
from jax import lax
from jax.experimental import pallas as pl
from jax.experimental.pallas import tpu as pltpu
from jax.sharding import PartitionSpec as P

EPSILON = 1e-06
LEARN_RATE = 0.01
MOMENTUM_BETA = 0.9
BF = jnp.bfloat16
F32 = jnp.float32
MIB = 1024 * 1024

SPOTS = [(x, t) for x in range(4) for t in range(4)]


def pairs(move):
    out = []
    for x, t in SPOTS:
        to_x, to_t = move(x, t)
        out.append((4 * x + t, 4 * (to_x % 4) + to_t))
    return out


X_UP = pairs(lambda x, t: (x + 1, t))
X_DOWN = pairs(lambda x, t: (x - 1, t))
X_FAR = pairs(lambda x, t: (x + 2, t))
X_NEXT = pairs(lambda x, t: (x ^ 1, t))
CORE = pairs(lambda x, t: (x, t ^ 1))
DEPTH = pairs(lambda x, t: (x, t ^ 2))
CROSS = pairs(lambda x, t: (x, t ^ 3))


def move(value, route):
    return lax.ppermute(value, "shard", route)


def in_order(t, pieces):
    out = []
    for a in range(4):
        value = pieces[a]
        for mine in (1, 2, 3):
            value = jnp.where(t == mine, pieces[a ^ mine], value)
        out.append(value)
    return out


def vmem(count):
    return [pl.BlockSpec(memory_space=pltpu.VMEM)] * count


def smem():
    return pl.BlockSpec(memory_space=pltpu.SMEM)


def after(value, *first):
    return lax.optimization_barrier((value,) + first)[0]


def call(body, ins, outs, scratch=(), limit=4, micros=1):
    return pl.pallas_call(
        body,
        out_shape=[jax.ShapeDtypeStruct(shape, kind) for shape, kind in outs],
        in_specs=[smem()] + vmem(ins),
        out_specs=vmem(len(outs)),
        scratch_shapes=list(scratch),
        compiler_params=pltpu.CompilerParams(vmem_limit_bytes=limit * MIB),
        cost_estimate=pl.CostEstimate(flops=micros * 1000000000, bytes_accessed=1000, transcendentals=0),
    )


def cut_body(spot, win, wout, table, *outs):
    for r in range(4):
        piece = outs[min(r, 2)]
        base = 80 if r == 3 else 0
        for block in range(4):
            start = pl.multiple_of((4 * block + spot[4 + r]) * 256, 256)
            piece[base : base + 64, 256 * block : 256 * block + 256] = win[:, pl.ds(start, 256)].astype(BF)
        for g in range(4):
            size = min(16, 54 - 16 * g)
            rows = table[16 * g : 16 * g + size, :]
            if size < 16:
                rows = jnp.concatenate([rows, jnp.zeros((8 - size, 64), F32), jnp.zeros((8, 64), F32)], axis=0)
            wide = jnp.concatenate([rows, jnp.zeros((16, 64), F32)], axis=1)
            piece[base + 64 : base + 80, 128 * g : 128 * g + 128] = wide.astype(BF)
        piece[base + 64 : base + 80, 512:1024] = jnp.zeros((16, 512), BF)
    outs[3][...] = wout[...].astype(BF)


def cut(spot, win, wout, table):
    return call(cut_body, 3, [((80, 1024), BF)] * 2 + [((160, 1024), BF), ((256, 1024), BF)], limit=6)(spot, win, wout, table)


def ahead_body(spot, param, moment, *outs):
    for r in range(4):
        piece = outs[min(r, 2)]
        base = 64 if r == 3 else 0
        for block in range(4):
            lanes = pl.ds(pl.multiple_of((4 * block + spot[4 + r]) * 256, 256), 256)
            value = param[:, lanes] - (LEARN_RATE * MOMENTUM_BETA) * moment[:, lanes]
            piece[base : base + 64, 256 * block : 256 * block + 256] = value.astype(BF)


def ahead(spot, param, moment):
    return call(ahead_body, 2, [((64, 1024), BF)] * 2 + [((128, 1024), BF)], limit=8)(spot, param, moment)


def join_body(spot, own, by_depth, both, bias, joined, tail):
    pieces = (own, both.at[0:80], by_depth.at[0:80], both.at[80:160])
    for r in range(4):
        joined[pl.ds(pl.multiple_of(64 * spot[4 + r], 64), 64), :] = pieces[r][0:64, :]
    for g in range(4):
        parts = [pieces[r][64:80, 128 * g : 128 * g + 64].astype(F32) for r in range(4)]
        for a in range(4):
            value = parts[0]
            for r in (1, 2, 3):
                value = jnp.where(spot[4 + r] == a, parts[r], value)
            tail[:, 256 * g + 64 * a : 256 * g + 64 * a + 64] = value
    tail[6:7, 768:1024] = bias[...]
    joined[256:272, :] = tail[...].astype(BF)


def join(spot, own, by_depth, both, bias):
    return call(join_body, 4, [((272, 1024), BF)], [pltpu.VMEM((16, 1024), F32)])(spot, own, by_depth, both, bias)[0]


def spans(rows):
    return [(start, min(112, rows - start)) for start in range(0, rows, 112)]


def norm_body(spot, own, near, *refs):
    packs = refs[0:4]
    normal_out, normed, inverse, table, wide, spatial = refs[4:]
    for k in range(4):
        lanes = pl.ds(pl.multiple_of(256 * spot[k], 256), 256)
        for g in range(4):
            table[16 * g : 16 * g + 16, lanes] = packs[k][:, 256 * g : 256 * g + 256].astype(F32)
    wide[0] = own[...].astype(F32)
    wide[1] = near[...].astype(F32)

    def lanes_step(at, carry):
        block = at % 8
        part = at // 8
        lanes = pl.ds(pl.multiple_of(block * 128, 128), 128)
        for i in range(7):
            acc = [jnp.broadcast_to(table[49:50, lanes], (8, 128)) for _ in range(7)]
            for r in range(7):
                row = i + r - 3
                if row < 0 or row > 6:
                    continue
                taps = [jnp.broadcast_to(table[7 * r + q : 7 * r + q + 1, lanes], (8, 128)) for q in range(7)]
                line = [wide[part, 8 * (7 * row + j) : 8 * (7 * row + j) + 8, lanes] for j in range(7)]
                for j in range(7):
                    for q in range(7):
                        if 0 <= j + q - 3 <= 6:
                            acc[j] = acc[j] + line[j + q - 3] * taps[q]
            for j in range(7):
                at_row = 8 * (7 * i + j)
                spatial[part, at_row : at_row + 8, lanes] = acc[j]
        return carry

    lax.fori_loop(0, 16, lanes_step, 0)
    gain = table[50:51, :]
    shift = table[51:52, :]
    for part in range(2):
        for start, size in spans(392):
            rows = slice(start, start + size)
            value = spatial[part, rows, :]
            centred = value - jnp.mean(value, axis=1, keepdims=True)
            scale = lax.rsqrt(jnp.mean(centred * centred, axis=1, keepdims=True) + EPSILON)
            unit = centred * scale
            shaped = (unit * gain + shift).astype(BF)
            inverse[part, rows, :] = jnp.broadcast_to(scale, (size, 128))
            for block in range(4):
                normed[part, block, rows, :] = unit[:, 256 * block : 256 * block + 256]
                normal_out[part, block, rows, :] = shaped[:, 256 * block : 256 * block + 256]


def norm(spot, own, near, packs):
    slabs = (2, 4, 392, 256)
    return call(
        norm_body,
        6,
        [(slabs, BF), (slabs, F32), ((2, 392, 128), F32), ((64, 1024), F32)],
        [pltpu.VMEM((2, 392, 1024), F32), pltpu.VMEM((2, 392, 1024), F32)],
        limit=10,
        micros=9,
    )(spot, own, near, *packs)


def normal_parts(value):
    bell = jnp.exp(-0.5 * value * value)
    t = 1.0 / (1.0 + (0.3275911 * 0.7071067811865476) * jnp.abs(value))
    poly = t * (
        0.5 * 0.254829592
        + t * (0.5 * -0.284496736 + t * (0.5 * 1.421413741 + t * (0.5 * -1.453152027 + t * (0.5 * 1.061405429))))
    )
    tail = poly * bell
    return jnp.where(value < 0.0, tail, 1.0 - tail), bell


def dot(left, right, left_dim, right_dim):
    return lax.dot_general(left, right, (((left_dim,), (right_dim,)), ((), ())), preferred_element_type=F32)


def forward_body(spot, *refs):
    normal = refs[0:2]
    win = refs[2:5] + (refs[10],)
    table = refs[7]
    activ = refs[8]
    slope = refs[9]
    win[3][0:128, :] = refs[5][128:256, :]
    win[3][128:256, :] = refs[6][128:256, :]

    def block_step(block, carry):
        lanes = pl.ds(pl.multiple_of(block * 256, 256), 256)
        bias = table[54:55, lanes]
        for r in range(4):
            pre = dot(normal[r % 2][r // 2, spot[0]], win[0][0:256, lanes], 1, 0)
            for k in range(1, 4):
                pre = pre + dot(normal[r % 2][r // 2, spot[k]], win[k][0:256, lanes], 1, 0)
            pre = pre + bias
            phi, bell = normal_parts(pre)
            activ[r, block] = (pre * phi).astype(BF)
            slope[r, block] = (phi + pre * bell * 0.3989422804014327).astype(BF)
        return carry

    lax.fori_loop(0, 4, block_step, 0)


def forward(spot, normal, win, far, table):
    return call(
        forward_body, 8, [((4, 4, 392, 256), BF)] * 2, [pltpu.VMEM((256, 1024), BF)], limit=8, micros=9
    )(spot, *normal, *win, *far, table)


def outer_body(spot, *refs):
    activ = refs[0]
    cot = refs[1:5]
    wout = refs[5:8]
    far = refs[8:10]
    table = refs[10]
    grads = refs[11:14]
    far_grads = refs[14:16]
    extras = refs[16]
    scale = table[53:54, :]
    grad_scale = jnp.sum(cot[0][...].astype(F32), axis=0, keepdims=True)
    extras[0:1, :] = grad_scale * scale
    grad_scale = grad_scale * table[52:53, :]
    for k in (3, 1, 2, 0):
        total = dot(activ[0, spot[k]], cot[0][...], 0, 0)
        for r in range(1, 4):
            total = total + dot(activ[r, spot[k]], cot[r][...], 0, 0)
        scaled = (total * scale).astype(BF)
        if k == 3:
            for h in range(2):
                rows = slice(128 * h, 128 * h + 128)
                grad_scale = grad_scale + jnp.sum(
                    total[rows] * far[h][0:128, :].astype(F32), axis=0, keepdims=True
                )
                far_grads[h][...] = scaled[rows]
        else:
            grad_scale = grad_scale + jnp.sum(total * wout[k][...].astype(F32), axis=0, keepdims=True)
            grads[k][...] = scaled
    extras[1:2, :] = grad_scale


def outer(spot, activ, cot, wout, far, table):
    out = call(
        outer_body,
        11,
        [((256, 1024), BF)] * 3 + [((128, 1024), BF)] * 2 + [((2, 1024), F32)],
        limit=8,
        micros=6,
    )(spot, activ, *cot, *wout, *far, table)
    return out[0:3], out[3:5], out[5]


def mix_body(spot, up, down, first, second, to_up, to_down):
    to_up[0:128, :] = (up[0:128, :].astype(F32) + first[...].astype(F32)).astype(BF)
    to_up[128:256, :] = up[128:256, :]
    to_down[0:128, :] = down[0:128, :]
    to_down[128:256, :] = (down[128:256, :].astype(F32) + second[...].astype(F32)).astype(BF)


def mix(spot, up, down, first, second):
    return call(mix_body, 4, [((256, 1024), BF)] * 2)(spot, up, down, first, second)


def back_body(spot, *refs):
    cot = refs[0:4]
    slope = refs[4]
    win = refs[5:8] + (refs[18],)
    wout = refs[8:11] + (refs[19],)
    far = refs[11:13]
    table = refs[13]
    pre_low = refs[14]
    home = refs[15]
    away = refs[16]
    bias = refs[17]
    low = refs[20]
    for h in range(2):
        wout[3][128 * h : 128 * h + 128, :] = far[h][0:128, :]
        win[3][128 * h : 128 * h + 128, :] = far[h][128:256, :]
    scale = table[53:54, :]
    for r in range(4):
        low[r] = (cot[r][...].astype(F32) * scale).astype(BF)
    for k in range(4):
        total = jnp.zeros((1, 256), F32)
        for r in range(4):
            grad = dot(low[r], wout[k][...], 1, 1) * slope[r, spot[k]].astype(F32)
            total = total + jnp.sum(grad, axis=0, keepdims=True)
            pre_low[r, spot[k]] = grad.astype(BF)
        bias[spot[k]] = total
    for k in range(4):
        for r in range(4):
            grad = dot(pre_low[r, 0], win[k][0:256, 0:256], 1, 1)
            for block in range(1, 4):
                grad = grad + dot(pre_low[r, block], win[k][0:256, 256 * block : 256 * block + 256], 1, 1)
            if r % 2:
                away[r // 2, spot[k]] = grad.astype(BF)
            else:
                home[r // 2, spot[k]] = grad.astype(BF)


def back(spot, cot, slope, win, wout, far, table):
    return call(
        back_body,
        14,
        [((4, 4, 392, 256), BF), ((2, 4, 392, 256), BF), ((2, 4, 392, 256), BF), ((4, 1, 256), F32)],
        [pltpu.VMEM((256, 1024), BF), pltpu.VMEM((256, 1024), BF), pltpu.VMEM((4, 392, 1024), BF)],
        limit=12,
        micros=10,
    )(spot, *cot, slope, *win, *wout, *far, table)


def weight_body(spot, *refs):
    normal = refs[0:2]
    pre_low = refs[2]
    grads = refs[3:6]
    far_grads = refs[6:8]
    for k in (3, 1, 2, 0):
        for block in range(4):
            cols = slice(256 * block, 256 * block + 256)
            total = dot(normal[0][0, spot[k]], pre_low[0, block], 0, 0)
            for r in range(1, 4):
                total = total + dot(normal[r % 2][r // 2, spot[k]], pre_low[r, block], 0, 0)
            if k == 3:
                for h in range(2):
                    far_grads[h][:, cols] = total[128 * h : 128 * h + 128].astype(BF)
            else:
                grads[k][:, cols] = total.astype(BF)


def weight(spot, normal, pre_low):
    out = call(
        weight_body,
        3,
        [((256, 1024), BF)] * 3 + [((128, 1024), BF)] * 2,
        limit=8,
        micros=20,
    )(spot, *normal, pre_low)
    return out[0:3], out[3:5]


def channel_body(spot, images, images_z, home, by_core, normed, inverse, table, bias, extras, *refs):
    total, out, wide, grid = refs
    gain_sum = [jnp.zeros((1, 256), F32) for _ in range(4)]
    shift_sum = [jnp.zeros((1, 256), F32) for _ in range(4)]
    dw_sum = [jnp.zeros((1, 256), F32) for _ in range(4)]
    for part, pixels in enumerate((images, images_z)):
        wide[part] = pixels[...].astype(F32)
        for start, size in spans(392):
            rows = slice(start, start + size)
            grads = []
            mean = jnp.zeros((size, 1), F32)
            cross = jnp.zeros((size, 1), F32)
            for block in range(4):
                cols = slice(256 * block, 256 * block + 256)
                grad = home[part, block, rows, :].astype(F32) + by_core[part, block, rows, :].astype(F32)
                unit = normed[part, block, rows, :]
                gain_sum[block] += jnp.sum(grad * unit, axis=0, keepdims=True)
                shift_sum[block] += jnp.sum(grad, axis=0, keepdims=True)
                scaled = grad * table[50:51, cols]
                mean += jnp.sum(scaled, axis=1, keepdims=True)
                cross += jnp.sum(scaled * unit, axis=1, keepdims=True)
                grads.append(scaled)
            mean = mean * (1.0 / 1024.0)
            cross = cross * (1.0 / 1024.0)
            factor = inverse[part, rows, 0:1]
            for block in range(4):
                cols = slice(256 * block, 256 * block + 256)
                value = factor * (grads[block] - mean - normed[part, block, rows, :] * cross)
                dw_sum[block] += jnp.sum(value, axis=0, keepdims=True)
                grid[part, rows, cols] = value
    for block in range(4):
        cols = slice(256 * block, 256 * block + 256)
        out[block, 49:50, :] = dw_sum[block]
        out[block, 50:51, :] = gain_sum[block]
        out[block, 51:52, :] = shift_sum[block]
        out[block, 52:54, :] = extras[:, cols]
        out[block, 54:55, :] = bias[block]
        out[block, 55:56, :] = jnp.zeros((1, 256), F32)

    def lanes_step(block, carry):
        lanes = pl.ds(pl.multiple_of(block * 128, 128), 128)
        to_lanes = pl.ds(pl.multiple_of((block % 2) * 128, 128), 128)
        for r in range(7):
            acc = [jnp.zeros((8, 128), F32) for _ in range(7)]
            for part in range(2):
                for i in range(7):
                    row = i + r - 3
                    if row < 0 or row > 6:
                        continue
                    line = [wide[part, 8 * (7 * row + j) : 8 * (7 * row + j) + 8, lanes] for j in range(7)]
                    grads = [grid[part, 8 * (7 * i + j) : 8 * (7 * i + j) + 8, lanes] for j in range(7)]
                    for q in range(7):
                        for j in range(7):
                            if 0 <= j + q - 3 <= 6:
                                acc[q] = acc[q] + line[j + q - 3] * grads[j]
            for q in range(7):
                out[block // 2, 7 * r + q : 7 * r + q + 1, to_lanes] = jnp.sum(acc[q], axis=0, keepdims=True)
        return carry

    lax.fori_loop(0, 8, lanes_step, 0)
    for turn in range(4):
        total[turn] = out[spot[8 + turn]]


def channel(spot, *operands):
    return call(
        channel_body,
        9,
        [((4, 56, 256), F32)],
        [pltpu.VMEM((4, 56, 256), F32), pltpu.VMEM((2, 392, 1024), F32), pltpu.VMEM((2, 392, 1024), F32)],
        limit=14,
        micros=2,
    )(spot, *operands)


def rows_body(spot, own, from_down, from_up, base_own, base_depth, base_both, *outs):
    bases = (base_own, base_both.at[0:64], base_depth.at[0:64], base_both.at[64:128])
    for r in range(4):
        rows = pl.ds(pl.multiple_of(64 * spot[4 + r], 64), 64)
        to = slice(64 * (r % 2), 64 * (r % 2) + 64)
        total = own[rows, :].astype(F32) + from_down[rows, :].astype(F32) + from_up[rows, :].astype(F32)
        outs[r // 2][to, :] = total.astype(BF)
        outs[2 + r // 2][to, :] = (bases[r][...].astype(F32) - LEARN_RATE * total).astype(BF)


def rows_of(spot, *operands):
    return call(rows_body, 6, [((128, 1024), BF)] * 4, limit=8)(spot, *operands)


def shift_body(spot, own, from_down, from_up, param, moment, new_moment, stepped, low):
    for start in range(0, 256, 64):
        rows = slice(start, start + 64)
        grad = own[rows, :].astype(F32) + from_down[rows, :].astype(F32) + from_up[rows, :].astype(F32)
        fresh = MOMENTUM_BETA * moment[rows, :] + grad
        moved = param[rows, :] - LEARN_RATE * fresh
        new_moment[rows, :] = fresh
        stepped[rows, :] = moved
        low[rows, :] = moved.astype(BF)


def shift(spot, *operands):
    return call(
        shift_body, 5, [((256, 1024), F32), ((256, 1024), F32), ((256, 1024), BF)], limit=8, micros=20
    )(spot, *operands)


def step_body(spot, *refs):
    here, by_depth, peer_here, peer_depth, by_core = refs[0:5]
    pieces = (here.at[0:64], by_core.at[0:64], by_depth.at[0:64], by_core.at[64:128])
    peers = (peer_here.at[0:64], by_core.at[128:192], peer_depth.at[0:64], by_core.at[192:256])
    param, moment, new_param, new_moment = refs[5:]
    for r in range(4):
        for block in range(4):
            lanes = pl.ds(pl.multiple_of((4 * block + spot[4 + r]) * 256, 256), 256)
            cols = slice(256 * block, 256 * block + 256)
            fresh = MOMENTUM_BETA * moment[:, lanes] + pieces[r][:, cols].astype(F32)
            after_step = param[:, lanes] - LEARN_RATE * fresh
            new_moment[:, lanes] = fresh
            new_param[:, lanes] = 0.5 * (after_step + peers[r][:, cols].astype(F32))


def step(spot, *operands):
    return call(step_body, 7, [((64, 4096), F32), ((64, 4096), F32)], limit=8)(spot, *operands)


def run(
    images,
    cotangent,
    weight_in,
    weight_out,
    channel_table,
    bias_in,
    moment_in,
):
    place = lax.axis_index("shard")
    x = place // 4
    t = place % 4
    spot = jnp.stack([x, (x + 1) % 4, (x + 3) % 4, (x + 2) % 4, t, t ^ 1, t ^ 2, t ^ 3, x, x ^ 1, x ^ 2, x ^ 3]).astype(jnp.int32)
    grid_images = images[0].transpose(1, 2, 0, 3).reshape(392, 1024)
    grid_cot = cotangent[0].transpose(1, 2, 0, 3).reshape(392, 1024)

    images_z = move(grid_images, DEPTH)
    cot_z = move(after(grid_cot, images_z), DEPTH)

    table_own = channel_table[0].T
    cut_own, cut_core, cut_away, wout_own = cut(spot, weight_in[0], weight_out[0], table_own)
    cut_depth = move(cut_away, DEPTH)
    wout_down = move(wout_own, X_UP)
    wout_up = move(wout_own, X_DOWN)
    cut_both = move(jnp.concatenate([cut_core, cut_depth[80:160]], axis=0), CORE)
    joined = join(spot, cut_own, cut_depth, after(cut_both, wout_down, wout_up), bias_in)
    joined_down = move(joined, X_UP)
    joined_up = move(joined, X_DOWN)
    tail_far = move(joined[256:272], X_FAR)
    packs = (joined[256:272], joined_up[256:272], joined_down[256:272], tail_far)
    far = (
        move(jnp.concatenate([wout_down[0:128], joined_down[0:128]], axis=0), X_UP),
        move(jnp.concatenate([wout_up[128:256], joined_up[128:256]], axis=0), X_DOWN),
    )
    win = (joined, joined_up, joined_down)
    wout = (wout_own, wout_up, wout_down)

    normal_own, normed, inverse, table = norm(spot, grid_images, images_z, packs)
    base_own, base_core, base_away = ahead(spot, weight_in[0], moment_in[0])
    base_depth = move(after(base_away, cot_z), DEPTH)
    normal = (normal_own, move(after(normal_own, *far, cot_z), CORE))
    activ, slope = forward(spot, normal, win, far, table)
    base_core, base_far, _ = lax.optimization_barrier((base_core, base_depth, slope))
    base_both = move(jnp.concatenate([base_core, base_far[64:128]], axis=0), CORE)
    cot = (grid_cot, move(after(grid_cot, images_z), CORE), cot_z, move(after(cot_z, normal_own), CORE))
    out_near, out_far, extras = outer(spot, activ, cot, wout, far, table)
    out_first = move(out_far[0], X_UP)
    out_second = move(out_far[1], X_DOWN)
    pre_low, home, away, grad_bias = back(spot, cot, after(slope, extras, base_both), win, wout, far, table)
    by_core = move(away, CORE)
    out_up, out_down = mix(spot, after(out_near[1], home), out_near[2], out_first, out_second)
    in_near, in_far = weight(spot, normal, after(pre_low, out_up))

    out_from_down = move(out_up, X_UP)
    out_from_up = move(out_down, X_DOWN)

    (small,) = channel(
        spot,
        grid_images,
        images_z,
        after(home, out_up),
        by_core,
        normed,
        inverse,
        table,
        grad_bias,
        extras,
    )
    in_up, in_down = mix(
        spot, after(in_near[1], small), in_near[2], move(in_far[0], X_UP), move(in_far[1], X_DOWN)
    )
    return (
        (spot, in_near[0], in_up, in_down, small, out_near[0], out_from_down, out_from_up)
        + (base_own, base_depth, base_both)
    )


def finish(
    level,
    spot,
    in_own,
    in_up,
    in_down,
    small,
    out_own,
    out_from_down,
    out_from_up,
    base_own,
    base_depth,
    base_both,
    weight_in,
    weight_out,
    channel_table,
    bias_in,
    moment_in,
    moment_out,
    moment_table,
    moment_bias,
):
    mask = 2**level
    swap = [(g, g ^ mask) for g in range(8)]

    def partner(value, turn):
        route = [
            (16 * g + 4 * x_at + t_at, 16 * (g ^ mask) + 4 * x_at + (t_at ^ turn))
            for g in range(8)
            for x_at, t_at in SPOTS
        ]
        return lax.ppermute(value, ("gossip", "shard"), route)

    def average(own, low):
        return 0.5 * (own + lax.ppermute(low, "gossip", swap).astype(F32))

    in_from_down = move(in_up, X_UP)
    in_from_up = move(in_down, X_DOWN)
    new_moment_out, stepped_out, low_out = shift(
        spot, out_own, out_from_down, out_from_up, weight_out[0], moment_out[0]
    )
    new_out = average(stepped_out, low_out)
    here, away, peer_here, peer_away = rows_of(
        spot, after(in_own, low_out), in_from_down, in_from_up, base_own, base_depth, base_both
    )
    by_depth = move(away, DEPTH)
    from_here = partner(peer_here, 0)
    from_depth = partner(peer_away, 2)
    across = move(
        jnp.concatenate(
            [here[64:128], after(by_depth, new_out)[64:128], from_here[64:128], from_depth[64:128]], axis=0
        ),
        CORE,
    )
    new_in, new_moment_in = step(
        spot, here, by_depth, from_here, from_depth, across, weight_in[0], moment_in[0]
    )

    t = spot[4]
    by_t = in_order(t, [small[:, :54, 64 * a : 64 * a + 64] for a in range(4)])
    half_t = jnp.stack(by_t[0:2]) + move(jnp.stack(by_t[2:4]).astype(BF), DEPTH).astype(F32)
    full_t = half_t[0] + move(half_t[1].astype(BF), CORE).astype(F32)
    both = jnp.concatenate([full_t, small[:, 54].reshape(4, 4, 64)], axis=1)
    half_x = both[0:2] + move(after(both[2:4].astype(BF), in_from_down), X_FAR).astype(F32)
    total = half_x[0] + move(half_x[1].astype(BF), X_NEXT).astype(F32)
    total_table = total[:54]
    total_bias = total[54:].reshape(1, 256)

    def update(param, moment, grad):
        fresh = MOMENTUM_BETA * moment + grad
        return fresh, param - LEARN_RATE * fresh

    new_moment_table, stepped_table = update(channel_table[0].T, moment_table[0].T, total_table)
    new_moment_bias, stepped_bias = update(bias_in, moment_bias, total_bias)
    stepped_small = jnp.concatenate([stepped_table, stepped_bias.reshape(4, 64)], axis=0)
    new_small = average(stepped_small, stepped_small.astype(BF))
    return (
        new_in[None],
        new_out[None],
        new_small[:54].T[None],
        new_small[54:].reshape(1, 256),
        new_moment_in[None],
        new_moment_out[None],
        new_moment_table.T[None],
        new_moment_bias,
    )


def on_device(*args):
    levels = lax.axis_size("gossip").bit_length() - 1
    middle = run(*args[:7])
    branches = [partial(finish, level) for level in range(levels)]
    return lax.switch(args[-1][0] % levels, branches, *middle, *args[2:10])


def solution(mesh):
    in_specs = (
        P("gossip", "shard", None, None, None),
        P("gossip", "shard", None, None, None),
        P("gossip", "shard", None),
        P("gossip", "shard", None),
        P("gossip", "shard", None),
        P("gossip", "shard"),
        P("gossip", "shard", None),
        P("gossip", "shard", None),
        P("gossip", "shard", None),
        P("gossip", "shard"),
        P(),
    )
    out_specs = (
        P("gossip", "shard", None),
        P("gossip", "shard", None),
        P("gossip", "shard", None),
        P("gossip", "shard"),
        P("gossip", "shard", None),
        P("gossip", "shard", None),
        P("gossip", "shard", None),
        P("gossip", "shard"),
    )
    return jax.shard_map(
        on_device, mesh=mesh, in_specs=in_specs, out_specs=out_specs, check_vma=False
    )
```

```python
from functools import partial

import jax
import jax.numpy as jnp
from jax import lax
from jax.experimental import pallas as pl
from jax.experimental.pallas import tpu as pltpu
from jax.sharding import PartitionSpec as P

EPSILON = 1e-06
LEARN_RATE = 0.01
MOMENTUM_BETA = 0.9
BF = jnp.bfloat16
F32 = jnp.float32
MIB = 1024 * 1024

SPOTS = [(x, t) for x in range(4) for t in range(4)]


def pairs(move):
    out = []
    for x, t in SPOTS:
        to_x, to_t = move(x, t)
        out.append((4 * x + t, 4 * (to_x % 4) + to_t))
    return out


X_UP = pairs(lambda x, t: (x + 1, t))
X_DOWN = pairs(lambda x, t: (x - 1, t))
X_FAR = pairs(lambda x, t: (x + 2, t))
X_NEXT = pairs(lambda x, t: (x ^ 1, t))
CORE = pairs(lambda x, t: (x, t ^ 1))
DEPTH = pairs(lambda x, t: (x, t ^ 2))
CROSS = pairs(lambda x, t: (x, t ^ 3))


def move(value, route):
    return lax.ppermute(value, "shard", route)


def in_order(t, pieces):
    out = []
    for a in range(4):
        value = pieces[a]
        for mine in (1, 2, 3):
            value = jnp.where(t == mine, pieces[a ^ mine], value)
        out.append(value)
    return out


def vmem(count):
    return [pl.BlockSpec(memory_space=pltpu.VMEM)] * count


def smem():
    return pl.BlockSpec(memory_space=pltpu.SMEM)


def after(value, *first):
    return lax.optimization_barrier((value,) + first)[0]


def call(body, ins, outs, scratch=(), limit=4, micros=1):
    return pl.pallas_call(
        body,
        out_shape=[jax.ShapeDtypeStruct(shape, kind) for shape, kind in outs],
        in_specs=[smem()] + vmem(ins),
        out_specs=vmem(len(outs)),
        scratch_shapes=list(scratch),
        compiler_params=pltpu.CompilerParams(vmem_limit_bytes=limit * MIB),
        cost_estimate=pl.CostEstimate(flops=micros * 1000000000, bytes_accessed=1000, transcendentals=0),
    )


def whole(shape):
    return pl.BlockSpec(shape, lambda step: (0,) * len(shape), pipeline_mode=pl.Buffered(buffer_count=1))


def piped(body, outs, scratch=(), limit=4, micros=1):
    def run_kernel(spot, *operands):
        return pl.pallas_call(
            body,
            grid=(1,),
            out_shape=[jax.ShapeDtypeStruct(shape, kind) for shape, kind in outs],
            in_specs=[smem()] + [whole(operand.shape) for operand in operands],
            out_specs=[whole(shape) for shape, _ in outs],
            scratch_shapes=list(scratch),
            compiler_params=pltpu.CompilerParams(vmem_limit_bytes=limit * MIB),
            cost_estimate=pl.CostEstimate(flops=micros * 1000000000, bytes_accessed=1000, transcendentals=0),
        )(spot, *operands)

    return run_kernel


def cut_body(spot, win, wout, table, *outs):
    for r in range(4):
        piece = outs[min(r, 2)]
        base = 80 if r == 3 else 0
        for block in range(4):
            start = pl.multiple_of((4 * block + spot[4 + r]) * 256, 256)
            piece[base : base + 64, 256 * block : 256 * block + 256] = win[:, pl.ds(start, 256)].astype(BF)
        for g in range(4):
            size = min(16, 54 - 16 * g)
            rows = table[16 * g : 16 * g + size, :]
            if size < 16:
                rows = jnp.concatenate([rows, jnp.zeros((8 - size, 64), F32), jnp.zeros((8, 64), F32)], axis=0)
            wide = jnp.concatenate([rows, jnp.zeros((16, 64), F32)], axis=1)
            piece[base + 64 : base + 80, 128 * g : 128 * g + 128] = wide.astype(BF)
        piece[base + 64 : base + 80, 512:1024] = jnp.zeros((16, 512), BF)
    outs[3][...] = wout[...].astype(BF)


def cut(spot, win, wout, table):
    return call(cut_body, 3, [((80, 1024), BF)] * 2 + [((160, 1024), BF), ((256, 1024), BF)], limit=6)(spot, win, wout, table)


def ahead_body(spot, param, moment, *outs):
    for r in range(4):
        piece = outs[min(r, 2)]
        base = 64 if r == 3 else 0
        for block in range(4):
            lanes = pl.ds(pl.multiple_of((4 * block + spot[4 + r]) * 256, 256), 256)
            value = param[:, lanes] - (LEARN_RATE * MOMENTUM_BETA) * moment[:, lanes]
            piece[base : base + 64, 256 * block : 256 * block + 256] = value.astype(BF)


def ahead(spot, param, moment):
    return call(ahead_body, 2, [((64, 1024), BF)] * 2 + [((128, 1024), BF)], limit=8)(spot, param, moment)


def join_body(spot, own, by_depth, both, bias, joined, tail):
    pieces = (own, both.at[0:80], by_depth.at[0:80], both.at[80:160])
    for r in range(4):
        joined[pl.ds(pl.multiple_of(64 * spot[4 + r], 64), 64), :] = pieces[r][0:64, :]
    for g in range(4):
        parts = [pieces[r][64:80, 128 * g : 128 * g + 64].astype(F32) for r in range(4)]
        for a in range(4):
            value = parts[0]
            for r in (1, 2, 3):
                value = jnp.where(spot[4 + r] == a, parts[r], value)
            tail[:, 256 * g + 64 * a : 256 * g + 64 * a + 64] = value
    tail[6:7, 768:1024] = bias[...]
    joined[256:272, :] = tail[...].astype(BF)


def join(spot, own, by_depth, both, bias):
    return call(join_body, 4, [((272, 1024), BF)], [pltpu.VMEM((16, 1024), F32)])(spot, own, by_depth, both, bias)[0]


def spans(rows):
    return [(start, min(112, rows - start)) for start in range(0, rows, 112)]


def norm_body(spot, own, near, *refs):
    packs = refs[0:4]
    normal_out, normed, inverse, table, wide, spatial = refs[4:]
    for k in range(4):
        lanes = pl.ds(pl.multiple_of(256 * spot[k], 256), 256)
        for g in range(4):
            table[16 * g : 16 * g + 16, lanes] = packs[k][:, 256 * g : 256 * g + 256].astype(F32)
    wide[0] = own[...].astype(F32)
    wide[1] = near[...].astype(F32)

    def lanes_step(at, carry):
        block = at % 8
        part = at // 8
        lanes = pl.ds(pl.multiple_of(block * 128, 128), 128)
        for i in range(7):
            acc = [jnp.broadcast_to(table[49:50, lanes], (8, 128)) for _ in range(7)]
            for r in range(7):
                row = i + r - 3
                if row < 0 or row > 6:
                    continue
                taps = [jnp.broadcast_to(table[7 * r + q : 7 * r + q + 1, lanes], (8, 128)) for q in range(7)]
                line = [wide[part, 8 * (7 * row + j) : 8 * (7 * row + j) + 8, lanes] for j in range(7)]
                for j in range(7):
                    for q in range(7):
                        if 0 <= j + q - 3 <= 6:
                            acc[j] = acc[j] + line[j + q - 3] * taps[q]
            for j in range(7):
                at_row = 8 * (7 * i + j)
                spatial[part, at_row : at_row + 8, lanes] = acc[j]
        return carry

    lax.fori_loop(0, 16, lanes_step, 0)
    gain = table[50:51, :]
    shift = table[51:52, :]
    for part in range(2):
        for start, size in spans(392):
            rows = slice(start, start + size)
            value = spatial[part, rows, :]
            centred = value - jnp.mean(value, axis=1, keepdims=True)
            scale = lax.rsqrt(jnp.mean(centred * centred, axis=1, keepdims=True) + EPSILON)
            unit = centred * scale
            shaped = (unit * gain + shift).astype(BF)
            inverse[part, rows, :] = jnp.broadcast_to(scale, (size, 128))
            for block in range(4):
                normed[part, block, rows, :] = unit[:, 256 * block : 256 * block + 256].astype(BF)
                normal_out[part, block, rows, :] = shaped[:, 256 * block : 256 * block + 256]


def norm(spot, own, near, packs):
    slabs = (2, 4, 392, 256)
    return call(
        norm_body,
        6,
        [(slabs, BF), (slabs, BF), ((2, 392, 128), F32), ((64, 1024), F32)],
        [pltpu.VMEM((2, 392, 1024), F32), pltpu.VMEM((2, 392, 1024), F32)],
        limit=10,
        micros=9,
    )(spot, own, near, *packs)


def normal_parts(value):
    bell = jnp.exp(-0.5 * value * value)
    t = 1.0 / (1.0 + (0.3275911 * 0.7071067811865476) * jnp.abs(value))
    poly = t * (
        0.5 * 0.254829592
        + t * (0.5 * -0.284496736 + t * (0.5 * 1.421413741 + t * (0.5 * -1.453152027 + t * (0.5 * 1.061405429))))
    )
    tail = poly * bell
    return jnp.where(value < 0.0, tail, 1.0 - tail), bell


def dot(left, right, left_dim, right_dim):
    return lax.dot_general(left, right, (((left_dim,), (right_dim,)), ((), ())), preferred_element_type=F32)


def forward_body(spot, *refs):
    normal = refs[0:2]
    win = refs[2:5] + (refs[10],)
    table = refs[7]
    activ = refs[8]
    slope = refs[9]
    win[3][0:128, :] = refs[5][128:256, :]
    win[3][128:256, :] = refs[6][128:256, :]

    def block_step(block, carry):
        lanes = pl.ds(pl.multiple_of(block * 256, 256), 256)
        bias = table[54:55, lanes]
        for r in range(4):
            pre = dot(normal[r % 2][r // 2, spot[0]], win[0][0:256, lanes], 1, 0)
            for k in range(1, 4):
                pre = pre + dot(normal[r % 2][r // 2, spot[k]], win[k][0:256, lanes], 1, 0)
            pre = pre + bias
            phi, bell = normal_parts(pre)
            activ[r, block] = (pre * phi).astype(BF)
            slope[r, block] = (phi + pre * bell * 0.3989422804014327).astype(BF)
        return carry

    lax.fori_loop(0, 4, block_step, 0)


def forward(spot, normal, win, far, table):
    return call(
        forward_body, 8, [((4, 4, 392, 256), BF)] * 2, [pltpu.VMEM((256, 1024), BF)], limit=8, micros=9
    )(spot, *normal, *win, *far, table)


def outer_body(spot, *refs):
    activ = refs[0]
    cot = refs[1:5]
    wout = refs[5:8]
    far = refs[8:10]
    table = refs[10]
    grads = refs[11:14]
    far_grads = refs[14:16]
    extras = refs[16]
    scale = table[53:54, :]
    grad_scale = jnp.sum(cot[0][...].astype(F32), axis=0, keepdims=True)
    extras[0:1, :] = grad_scale * scale
    grad_scale = grad_scale * table[52:53, :]
    for k in (3, 1, 2, 0):
        total = dot(activ[0, spot[k]], cot[0][...], 0, 0)
        for r in range(1, 4):
            total = total + dot(activ[r, spot[k]], cot[r][...], 0, 0)
        scaled = (total * scale).astype(BF)
        if k == 3:
            for h in range(2):
                rows = slice(128 * h, 128 * h + 128)
                grad_scale = grad_scale + jnp.sum(
                    total[rows] * far[h][0:128, :].astype(F32), axis=0, keepdims=True
                )
                far_grads[h][...] = scaled[rows]
        else:
            grad_scale = grad_scale + jnp.sum(total * wout[k][...].astype(F32), axis=0, keepdims=True)
            grads[k][...] = scaled
    extras[1:2, :] = grad_scale


def outer(spot, activ, cot, wout, far, table):
    out = call(
        outer_body,
        11,
        [((256, 1024), BF)] * 3 + [((128, 1024), BF)] * 2 + [((2, 1024), F32)],
        limit=8,
        micros=6,
    )(spot, activ, *cot, *wout, *far, table)
    return out[0:3], out[3:5], out[5]


def mix_body(spot, up, down, first, second, to_up, to_down):
    to_up[0:128, :] = (up[0:128, :].astype(F32) + first[...].astype(F32)).astype(BF)
    to_up[128:256, :] = up[128:256, :]
    to_down[0:128, :] = down[0:128, :]
    to_down[128:256, :] = (down[128:256, :].astype(F32) + second[...].astype(F32)).astype(BF)


def mix(spot, up, down, first, second):
    return call(mix_body, 4, [((256, 1024), BF)] * 2)(spot, up, down, first, second)


def mix_piped(spot, up, down, first, second):
    return piped(mix_body, [((256, 1024), BF)] * 2, limit=6)(spot, up, down, first, second)


def back_body(spot, *refs):
    cot = refs[0:4]
    slope = refs[4]
    win = refs[5:8] + (refs[18],)
    wout = refs[8:11] + (refs[19],)
    far = refs[11:13]
    table = refs[13]
    pre_low = refs[14]
    home = refs[15]
    away = refs[16]
    bias = refs[17]
    low = refs[20]
    for h in range(2):
        wout[3][128 * h : 128 * h + 128, :] = far[h][0:128, :]
        win[3][128 * h : 128 * h + 128, :] = far[h][128:256, :]
    scale = table[53:54, :]
    for r in range(4):
        low[r] = (cot[r][...].astype(F32) * scale).astype(BF)
    for k in range(4):
        total = jnp.zeros((1, 256), F32)
        for r in range(4):
            grad = dot(low[r], wout[k][...], 1, 1) * slope[r, spot[k]].astype(F32)
            total = total + jnp.sum(grad, axis=0, keepdims=True)
            pre_low[r, spot[k]] = grad.astype(BF)
        bias[spot[k]] = total
    for k in range(4):
        for r in range(4):
            grad = dot(pre_low[r, 0], win[k][0:256, 0:256], 1, 1)
            for block in range(1, 4):
                grad = grad + dot(pre_low[r, block], win[k][0:256, 256 * block : 256 * block + 256], 1, 1)
            if r % 2:
                away[r // 2, spot[k]] = grad.astype(BF)
            else:
                home[r // 2, spot[k]] = grad.astype(BF)


def back(spot, cot, slope, win, wout, far, table):
    return call(
        back_body,
        14,
        [((4, 4, 392, 256), BF), ((2, 4, 392, 256), BF), ((2, 4, 392, 256), BF), ((4, 1, 256), F32)],
        [pltpu.VMEM((256, 1024), BF), pltpu.VMEM((256, 1024), BF), pltpu.VMEM((4, 392, 1024), BF)],
        limit=12,
        micros=10,
    )(spot, *cot, slope, *win, *wout, *far, table)


def weight_body(spot, *refs):
    normal = refs[0:2]
    pre_low = refs[2]
    grads = refs[3:6]
    far_grads = refs[6:8]
    for k in (3, 1, 2, 0):
        for block in range(4):
            cols = slice(256 * block, 256 * block + 256)
            total = dot(normal[0][0, spot[k]], pre_low[0, block], 0, 0)
            for r in range(1, 4):
                total = total + dot(normal[r % 2][r // 2, spot[k]], pre_low[r, block], 0, 0)
            if k == 3:
                for h in range(2):
                    far_grads[h][:, cols] = total[128 * h : 128 * h + 128].astype(BF)
            else:
                grads[k][:, cols] = total.astype(BF)


def weight(spot, normal, pre_low):
    out = call(
        weight_body,
        3,
        [((256, 1024), BF)] * 3 + [((128, 1024), BF)] * 2,
        limit=6,
        micros=20,
    )(spot, *normal, pre_low)
    return out[0:3], out[3:5]


def channel_body(spot, images, images_z, home, by_core, normed, inverse, table, bias, extras, *refs):
    total, out, wide, grid = refs
    gain_sum = [jnp.zeros((1, 256), F32) for _ in range(4)]
    shift_sum = [jnp.zeros((1, 256), F32) for _ in range(4)]
    dw_sum = [jnp.zeros((1, 256), F32) for _ in range(4)]
    for part, pixels in enumerate((images, images_z)):
        wide[part] = pixels[...].astype(F32)
        for start, size in spans(392):
            rows = slice(start, start + size)
            grads = []
            mean = jnp.zeros((size, 1), F32)
            cross = jnp.zeros((size, 1), F32)
            for block in range(4):
                cols = slice(256 * block, 256 * block + 256)
                grad = home[part, block, rows, :].astype(F32) + by_core[part, block, rows, :].astype(F32)
                unit = normed[part, block, rows, :].astype(F32)
                gain_sum[block] += jnp.sum(grad * unit, axis=0, keepdims=True)
                shift_sum[block] += jnp.sum(grad, axis=0, keepdims=True)
                scaled = grad * table[50:51, cols]
                mean += jnp.sum(scaled, axis=1, keepdims=True)
                cross += jnp.sum(scaled * unit, axis=1, keepdims=True)
                grads.append(scaled)
            mean = mean * (1.0 / 1024.0)
            cross = cross * (1.0 / 1024.0)
            factor = inverse[part, rows, 0:1]
            for block in range(4):
                cols = slice(256 * block, 256 * block + 256)
                value = factor * (grads[block] - mean - normed[part, block, rows, :].astype(F32) * cross)
                dw_sum[block] += jnp.sum(value, axis=0, keepdims=True)
                grid[part, rows, cols] = value
    for block in range(4):
        cols = slice(256 * block, 256 * block + 256)
        out[block, 49:50, :] = dw_sum[block]
        out[block, 50:51, :] = gain_sum[block]
        out[block, 51:52, :] = shift_sum[block]
        out[block, 52:54, :] = extras[:, cols]
        out[block, 54:55, :] = bias[block]
        out[block, 55:56, :] = jnp.zeros((1, 256), F32)

    def lanes_step(block, carry):
        lanes = pl.ds(pl.multiple_of(block * 128, 128), 128)
        to_lanes = pl.ds(pl.multiple_of((block % 2) * 128, 128), 128)
        for r in range(7):
            acc = [jnp.zeros((8, 128), F32) for _ in range(7)]
            for part in range(2):
                for i in range(7):
                    row = i + r - 3
                    if row < 0 or row > 6:
                        continue
                    line = [wide[part, 8 * (7 * row + j) : 8 * (7 * row + j) + 8, lanes] for j in range(7)]
                    grads = [grid[part, 8 * (7 * i + j) : 8 * (7 * i + j) + 8, lanes] for j in range(7)]
                    for q in range(7):
                        for j in range(7):
                            if 0 <= j + q - 3 <= 6:
                                acc[q] = acc[q] + line[j + q - 3] * grads[j]
            for q in range(7):
                out[block // 2, 7 * r + q : 7 * r + q + 1, to_lanes] = jnp.sum(acc[q], axis=0, keepdims=True)
        return carry

    lax.fori_loop(0, 8, lanes_step, 0)
    for turn in range(4):
        total[turn] = out[spot[8 + turn]]


def channel(spot, *operands):
    return piped(
        channel_body,
        [((4, 56, 256), F32)],
        [pltpu.VMEM((4, 56, 256), F32), pltpu.VMEM((2, 392, 1024), F32), pltpu.VMEM((2, 392, 1024), F32)],
        limit=56,
        micros=2,
    )(spot, *operands)


def rows_body(spot, own, from_down, from_up, base_own, base_depth, base_both, *outs):
    bases = (base_own, base_both.at[0:64], base_depth.at[0:64], base_both.at[64:128])
    for r in range(4):
        rows = pl.ds(pl.multiple_of(64 * spot[4 + r], 64), 64)
        to = slice(64 * (r % 2), 64 * (r % 2) + 64)
        total = own[rows, :].astype(F32) + from_down[rows, :].astype(F32) + from_up[rows, :].astype(F32)
        outs[r // 2][to, :] = total.astype(BF)
        outs[2 + r // 2][to, :] = (bases[r][...].astype(F32) - LEARN_RATE * total).astype(BF)


def rows_of(spot, *operands):
    return call(rows_body, 6, [((128, 1024), BF)] * 4, limit=8)(spot, *operands)


def shift_body(spot, own, from_down, from_up, param, moment, new_moment, stepped, low):
    for start in range(0, 256, 64):
        rows = slice(start, start + 64)
        grad = own[rows, :].astype(F32) + from_down[rows, :].astype(F32) + from_up[rows, :].astype(F32)
        fresh = MOMENTUM_BETA * moment[rows, :] + grad
        moved = param[rows, :] - LEARN_RATE * fresh
        new_moment[rows, :] = fresh
        stepped[rows, :] = moved
        low[rows, :] = moved.astype(BF)


def shift(spot, *operands):
    return call(
        shift_body, 5, [((256, 1024), F32), ((256, 1024), F32), ((256, 1024), BF)], limit=8, micros=20
    )(spot, *operands)


def step_body(spot, *refs):
    here, by_depth, peer_here, peer_depth, by_core = refs[0:5]
    pieces = (here.at[0:64], by_core.at[0:64], by_depth.at[0:64], by_core.at[64:128])
    peers = (peer_here.at[0:64], by_core.at[128:192], peer_depth.at[0:64], by_core.at[192:256])
    param, moment, new_param, new_moment = refs[5:]
    for r in range(4):
        for block in range(4):
            lanes = pl.ds(pl.multiple_of((4 * block + spot[4 + r]) * 256, 256), 256)
            cols = slice(256 * block, 256 * block + 256)
            fresh = MOMENTUM_BETA * moment[:, lanes] + pieces[r][:, cols].astype(F32)
            after_step = param[:, lanes] - LEARN_RATE * fresh
            new_moment[:, lanes] = fresh
            new_param[:, lanes] = 0.5 * (after_step + peers[r][:, cols].astype(F32))


def step(spot, *operands):
    return call(step_body, 7, [((64, 4096), F32), ((64, 4096), F32)], limit=8)(spot, *operands)


def run(
    images,
    cotangent,
    weight_in,
    weight_out,
    channel_table,
    bias_in,
    moment_in,
):
    place = lax.axis_index("shard")
    x = place // 4
    t = place % 4
    spot = jnp.stack([x, (x + 1) % 4, (x + 3) % 4, (x + 2) % 4, t, t ^ 1, t ^ 2, t ^ 3, x, x ^ 1, x ^ 2, x ^ 3]).astype(jnp.int32)
    grid_images = images[0].transpose(1, 2, 0, 3).reshape(392, 1024)
    grid_cot = cotangent[0].transpose(1, 2, 0, 3).reshape(392, 1024)

    images_z = move(grid_images, DEPTH)
    cot_z = move(after(grid_cot, images_z), DEPTH)

    table_own = channel_table[0].T
    cut_own, cut_core, cut_away, wout_own = cut(spot, weight_in[0], weight_out[0], table_own)
    cut_depth = move(cut_away, DEPTH)
    wout_down = move(wout_own, X_UP)
    wout_up = move(wout_own, X_DOWN)
    cut_both = move(jnp.concatenate([cut_core, cut_depth[80:160]], axis=0), CORE)
    joined = join(spot, cut_own, cut_depth, after(cut_both, wout_down, wout_up), bias_in)
    joined_down = move(joined, X_UP)
    joined_up = move(joined, X_DOWN)
    tail_far = move(joined[256:272], X_FAR)
    packs = (joined[256:272], joined_up[256:272], joined_down[256:272], tail_far)
    far = (
        move(jnp.concatenate([wout_down[0:128], joined_down[0:128]], axis=0), X_UP),
        move(jnp.concatenate([wout_up[128:256], joined_up[128:256]], axis=0), X_DOWN),
    )
    win = (joined, joined_up, joined_down)
    wout = (wout_own, wout_up, wout_down)

    normal_own, normed, inverse, table = norm(spot, grid_images, images_z, packs)
    base_own, base_core, base_away = ahead(spot, weight_in[0], moment_in[0])
    base_depth = move(after(base_away, cot_z), DEPTH)
    normal = (normal_own, move(after(normal_own, *far, cot_z), CORE))
    activ, slope = forward(spot, normal, win, far, table)
    base_core, base_far, _ = lax.optimization_barrier((base_core, base_depth, slope))
    base_both = move(jnp.concatenate([base_core, base_far[64:128]], axis=0), CORE)
    cot = (grid_cot, move(after(grid_cot, images_z), CORE), cot_z, move(after(cot_z, normal_own), CORE))
    out_near, out_far, extras = outer(spot, activ, cot, wout, far, table)
    out_first = move(out_far[0], X_UP)
    out_second = move(out_far[1], X_DOWN)
    pre_low, home, away, grad_bias = back(spot, cot, after(slope, extras, base_both), win, wout, far, table)
    by_core = move(away, CORE)
    out_up, out_down = mix(spot, after(out_near[1], home), out_near[2], out_first, out_second)
    in_near, in_far = weight(spot, normal, after(pre_low, out_up))

    out_from_down = move(out_up, X_UP)
    out_from_up = move(out_down, X_DOWN)

    (small,) = channel(
        spot,
        grid_images,
        images_z,
        after(home, out_up),
        by_core,
        normed,
        inverse,
        table,
        grad_bias,
        extras,
    )
    in_up, in_down = mix_piped(
        spot, after(in_near[1], small), in_near[2], move(in_far[0], X_UP), move(in_far[1], X_DOWN)
    )
    return (
        (spot, in_near[0], in_up, in_down, small, out_near[0], out_from_down, out_from_up)
        + (base_own, base_depth, base_both)
    )


def finish(
    level,
    spot,
    in_own,
    in_up,
    in_down,
    small,
    out_own,
    out_from_down,
    out_from_up,
    base_own,
    base_depth,
    base_both,
    weight_in,
    weight_out,
    channel_table,
    bias_in,
    moment_in,
    moment_out,
    moment_table,
    moment_bias,
):
    mask = 2**level
    swap = [(g, g ^ mask) for g in range(8)]

    def partner(value, turn):
        route = [
            (16 * g + 4 * x_at + t_at, 16 * (g ^ mask) + 4 * x_at + (t_at ^ turn))
            for g in range(8)
            for x_at, t_at in SPOTS
        ]
        return lax.ppermute(value, ("gossip", "shard"), route)

    def average(own, low):
        return 0.5 * (own + lax.ppermute(low, "gossip", swap).astype(F32))

    in_from_down = move(in_up, X_UP)
    in_from_up = move(in_down, X_DOWN)
    new_moment_out, stepped_out, low_out = shift(
        spot, out_own, out_from_down, out_from_up, weight_out[0], moment_out[0]
    )
    new_out = average(stepped_out, low_out)
    here, away, peer_here, peer_away = rows_of(
        spot, after(in_own, low_out), in_from_down, in_from_up, base_own, base_depth, base_both
    )
    by_depth = move(away, DEPTH)
    from_here = partner(peer_here, 0)
    from_depth = partner(peer_away, 2)
    across = move(
        jnp.concatenate(
            [here[64:128], after(by_depth, new_out)[64:128], from_here[64:128], from_depth[64:128]], axis=0
        ),
        CORE,
    )
    new_in, new_moment_in = step(
        spot, here, by_depth, from_here, from_depth, across, weight_in[0], moment_in[0]
    )

    t = spot[4]
    by_t = in_order(t, [small[:, :54, 64 * a : 64 * a + 64] for a in range(4)])
    half_t = jnp.stack(by_t[0:2]) + move(jnp.stack(by_t[2:4]).astype(BF), DEPTH).astype(F32)
    full_t = half_t[0] + move(half_t[1].astype(BF), CORE).astype(F32)
    both = jnp.concatenate([full_t, small[:, 54].reshape(4, 4, 64)], axis=1)
    half_x = both[0:2] + move(after(both[2:4].astype(BF), in_from_down), X_FAR).astype(F32)
    total = half_x[0] + move(half_x[1].astype(BF), X_NEXT).astype(F32)
    total_table = total[:54]
    total_bias = total[54:].reshape(1, 256)

    def update(param, moment, grad):
        fresh = MOMENTUM_BETA * moment + grad
        return fresh, param - LEARN_RATE * fresh

    new_moment_table, stepped_table = update(channel_table[0].T, moment_table[0].T, total_table)
    new_moment_bias, stepped_bias = update(bias_in, moment_bias, total_bias)
    stepped_small = jnp.concatenate([stepped_table, stepped_bias.reshape(4, 64)], axis=0)
    new_small = average(stepped_small, stepped_small.astype(BF))
    return (
        new_in[None],
        new_out[None],
        new_small[:54].T[None],
        new_small[54:].reshape(1, 256),
        new_moment_in[None],
        new_moment_out[None],
        new_moment_table.T[None],
        new_moment_bias,
    )


def on_device(*args):
    levels = lax.axis_size("gossip").bit_length() - 1
    middle = run(*args[:7])
    branches = [partial(finish, level) for level in range(levels)]
    return lax.switch(args[-1][0] % levels, branches, *middle, *args[2:10])


def solution(mesh):
    in_specs = (
        P("gossip", "shard", None, None, None),
        P("gossip", "shard", None, None, None),
        P("gossip", "shard", None),
        P("gossip", "shard", None),
        P("gossip", "shard", None),
        P("gossip", "shard"),
        P("gossip", "shard", None),
        P("gossip", "shard", None),
        P("gossip", "shard", None),
        P("gossip", "shard"),
        P(),
    )
    out_specs = (
        P("gossip", "shard", None),
        P("gossip", "shard", None),
        P("gossip", "shard", None),
        P("gossip", "shard"),
        P("gossip", "shard", None),
        P("gossip", "shard", None),
        P("gossip", "shard", None),
        P("gossip", "shard"),
    )
    return jax.shard_map(
        on_device, mesh=mesh, in_specs=in_specs, out_specs=out_specs, check_vma=False
    )
```

```python
from functools import partial

import jax
import jax.numpy as jnp
from jax import lax
from jax.experimental import pallas as pl
from jax.experimental.pallas import tpu as pltpu
from jax.sharding import PartitionSpec as P

EPSILON = 1e-06
LEARN_RATE = 0.01
MOMENTUM_BETA = 0.9
BF = jnp.bfloat16
F32 = jnp.float32
MIB = 1024 * 1024

SPOTS = [(x, t) for x in range(4) for t in range(4)]


def pairs(move):
    out = []
    for x, t in SPOTS:
        to_x, to_t = move(x, t)
        out.append((4 * x + t, 4 * (to_x % 4) + to_t))
    return out


X_UP = pairs(lambda x, t: (x + 1, t))
X_DOWN = pairs(lambda x, t: (x - 1, t))
X_FAR = pairs(lambda x, t: (x + 2, t))
X_NEXT = pairs(lambda x, t: (x ^ 1, t))
CORE = pairs(lambda x, t: (x, t ^ 1))
DEPTH = pairs(lambda x, t: (x, t ^ 2))
CROSS = pairs(lambda x, t: (x, t ^ 3))


def move(value, route):
    return lax.ppermute(value, "shard", route)


def in_order(t, pieces):
    out = []
    for a in range(4):
        value = pieces[a]
        for mine in (1, 2, 3):
            value = jnp.where(t == mine, pieces[a ^ mine], value)
        out.append(value)
    return out


def vmem(count):
    return [pl.BlockSpec(memory_space=pltpu.VMEM)] * count


def smem():
    return pl.BlockSpec(memory_space=pltpu.SMEM)


def after(value, *first):
    return lax.optimization_barrier((value,) + first)[0]


def call(body, ins, outs, scratch=(), limit=4, micros=1):
    return pl.pallas_call(
        body,
        out_shape=[jax.ShapeDtypeStruct(shape, kind) for shape, kind in outs],
        in_specs=[smem()] + vmem(ins),
        out_specs=vmem(len(outs)),
        scratch_shapes=list(scratch),
        compiler_params=pltpu.CompilerParams(vmem_limit_bytes=limit * MIB),
        cost_estimate=pl.CostEstimate(flops=micros * 1000000000, bytes_accessed=1000, transcendentals=0),
    )


def whole(shape):
    return pl.BlockSpec(shape, lambda step: (0,) * len(shape), pipeline_mode=pl.Buffered(buffer_count=1))


def piped(body, outs, scratch=(), limit=4, micros=1):
    def run_kernel(spot, *operands):
        return pl.pallas_call(
            body,
            grid=(1,),
            out_shape=[jax.ShapeDtypeStruct(shape, kind) for shape, kind in outs],
            in_specs=[smem()] + [whole(operand.shape) for operand in operands],
            out_specs=[whole(shape) for shape, _ in outs],
            scratch_shapes=list(scratch),
            compiler_params=pltpu.CompilerParams(vmem_limit_bytes=limit * MIB),
            cost_estimate=pl.CostEstimate(flops=micros * 1000000000, bytes_accessed=1000, transcendentals=0),
        )(spot, *operands)

    return run_kernel


def cut_body(spot, win, wout, table, *outs):
    for r in range(4):
        piece = outs[min(r, 2)]
        base = 80 if r == 3 else 0
        for block in range(4):
            start = pl.multiple_of((4 * block + spot[4 + r]) * 256, 256)
            piece[base : base + 64, 256 * block : 256 * block + 256] = win[:, pl.ds(start, 256)].astype(BF)
        for g in range(4):
            size = min(16, 54 - 16 * g)
            rows = table[16 * g : 16 * g + size, :]
            if size < 16:
                rows = jnp.concatenate([rows, jnp.zeros((8 - size, 64), F32), jnp.zeros((8, 64), F32)], axis=0)
            wide = jnp.concatenate([rows, jnp.zeros((16, 64), F32)], axis=1)
            piece[base + 64 : base + 80, 128 * g : 128 * g + 128] = wide.astype(BF)
        piece[base + 64 : base + 80, 512:1024] = jnp.zeros((16, 512), BF)
    outs[3][...] = wout[...].astype(BF)


def cut(spot, win, wout, table):
    return call(cut_body, 3, [((80, 1024), BF)] * 2 + [((160, 1024), BF), ((256, 1024), BF)], limit=6)(spot, win, wout, table)


def ahead_body(spot, param, moment, *outs):
    for r in range(4):
        piece = outs[min(r, 2)]
        base = 64 if r == 3 else 0
        for block in range(4):
            lanes = pl.ds(pl.multiple_of((4 * block + spot[4 + r]) * 256, 256), 256)
            value = param[:, lanes] - (LEARN_RATE * MOMENTUM_BETA) * moment[:, lanes]
            piece[base : base + 64, 256 * block : 256 * block + 256] = value.astype(BF)


def ahead(spot, param, moment):
    return call(ahead_body, 2, [((64, 1024), BF)] * 2 + [((128, 1024), BF)], limit=8)(spot, param, moment)


def join_body(spot, own, by_depth, both, bias, joined, tail):
    pieces = (own, both.at[0:80], by_depth.at[0:80], both.at[80:160])
    for r in range(4):
        joined[pl.ds(pl.multiple_of(64 * spot[4 + r], 64), 64), :] = pieces[r][0:64, :]
    for g in range(4):
        parts = [pieces[r][64:80, 128 * g : 128 * g + 64].astype(F32) for r in range(4)]
        for a in range(4):
            value = parts[0]
            for r in (1, 2, 3):
                value = jnp.where(spot[4 + r] == a, parts[r], value)
            tail[:, 256 * g + 64 * a : 256 * g + 64 * a + 64] = value
    tail[6:7, 768:1024] = bias[...]
    joined[256:272, :] = tail[...].astype(BF)


def join(spot, own, by_depth, both, bias):
    return call(join_body, 4, [((272, 1024), BF)], [pltpu.VMEM((16, 1024), F32)])(spot, own, by_depth, both, bias)[0]


def spans(rows):
    return [(start, min(112, rows - start)) for start in range(0, rows, 112)]


def norm_body(spot, own, near, *refs):
    packs = refs[0:4]
    normal_out, normed, inverse, table, wide, spatial = refs[4:]
    for k in range(4):
        lanes = pl.ds(pl.multiple_of(256 * spot[k], 256), 256)
        for g in range(4):
            table[16 * g : 16 * g + 16, lanes] = packs[k][:, 256 * g : 256 * g + 256].astype(F32)
    wide[0] = own[...].astype(F32)
    wide[1] = near[...].astype(F32)

    def lanes_step(at, carry):
        block = at % 8
        part = at // 8
        lanes = pl.ds(pl.multiple_of(block * 128, 128), 128)
        for i in range(7):
            acc = [jnp.broadcast_to(table[49:50, lanes], (8, 128)) for _ in range(7)]
            for r in range(7):
                row = i + r - 3
                if row < 0 or row > 6:
                    continue
                taps = [jnp.broadcast_to(table[7 * r + q : 7 * r + q + 1, lanes], (8, 128)) for q in range(7)]
                line = [wide[part, 8 * (7 * row + j) : 8 * (7 * row + j) + 8, lanes] for j in range(7)]
                for j in range(7):
                    for q in range(7):
                        if 0 <= j + q - 3 <= 6:
                            acc[j] = acc[j] + line[j + q - 3] * taps[q]
            for j in range(7):
                at_row = 8 * (7 * i + j)
                spatial[part, at_row : at_row + 8, lanes] = acc[j]
        return carry

    lax.fori_loop(0, 16, lanes_step, 0)
    gain = table[50:51, :]
    shift = table[51:52, :]
    for part in range(2):
        for start, size in spans(392):
            rows = slice(start, start + size)
            value = spatial[part, rows, :]
            centred = value - jnp.mean(value, axis=1, keepdims=True)
            scale = lax.rsqrt(jnp.mean(centred * centred, axis=1, keepdims=True) + EPSILON)
            unit = centred * scale
            shaped = (unit * gain + shift).astype(BF)
            inverse[part, rows, :] = jnp.broadcast_to(scale, (size, 128))
            for block in range(4):
                normed[part, block, rows, :] = unit[:, 256 * block : 256 * block + 256].astype(BF)
                normal_out[part, block, rows, :] = shaped[:, 256 * block : 256 * block + 256]


def norm(spot, own, near, packs):
    slabs = (2, 4, 392, 256)
    return call(
        norm_body,
        6,
        [(slabs, BF), (slabs, BF), ((2, 392, 128), F32), ((64, 1024), F32)],
        [pltpu.VMEM((2, 392, 1024), F32), pltpu.VMEM((2, 392, 1024), F32)],
        limit=10,
        micros=9,
    )(spot, own, near, *packs)


def normal_parts(value):
    bell = jnp.exp(-0.5 * value * value)
    t = 1.0 / (1.0 + (0.3275911 * 0.7071067811865476) * jnp.abs(value))
    poly = t * (
        0.5 * 0.254829592
        + t * (0.5 * -0.284496736 + t * (0.5 * 1.421413741 + t * (0.5 * -1.453152027 + t * (0.5 * 1.061405429))))
    )
    tail = poly * bell
    return jnp.where(value < 0.0, tail, 1.0 - tail), bell


def dot(left, right, left_dim, right_dim):
    return lax.dot_general(left, right, (((left_dim,), (right_dim,)), ((), ())), preferred_element_type=F32)


def forward_body(spot, *refs):
    normal = refs[0:2]
    win = refs[2:5] + (refs[10],)
    table = refs[7]
    activ = refs[8]
    slope = refs[9]
    win[3][0:128, :] = refs[5][128:256, :]
    win[3][128:256, :] = refs[6][128:256, :]

    def block_step(block, carry):
        lanes = pl.ds(pl.multiple_of(block * 256, 256), 256)
        bias = table[54:55, lanes]
        for r in range(4):
            pre = dot(normal[r % 2][r // 2, spot[0]], win[0][0:256, lanes], 1, 0)
            for k in range(1, 4):
                pre = pre + dot(normal[r % 2][r // 2, spot[k]], win[k][0:256, lanes], 1, 0)
            pre = pre + bias
            phi, bell = normal_parts(pre)
            activ[r, block] = (pre * phi).astype(BF)
            slope[r, block] = (phi + pre * bell * 0.3989422804014327).astype(BF)
        return carry

    lax.fori_loop(0, 4, block_step, 0)


def forward(spot, normal, win, far, table):
    return call(
        forward_body, 8, [((4, 4, 392, 256), BF)] * 2, [pltpu.VMEM((256, 1024), BF)], limit=8, micros=9
    )(spot, *normal, *win, *far, table)


def outer_body(spot, *refs):
    activ = refs[0]
    cot = refs[1:5]
    wout = refs[5:8]
    far = refs[8:10]
    table = refs[10]
    grads = refs[11:14]
    far_grads = refs[14:16]
    extras = refs[16]
    scale = table[53:54, :]
    grad_scale = jnp.sum(cot[0][...].astype(F32), axis=0, keepdims=True)
    extras[0:1, :] = grad_scale * scale
    grad_scale = grad_scale * table[52:53, :]
    for k in (3, 1, 2, 0):
        total = dot(activ[0, spot[k]], cot[0][...], 0, 0)
        for r in range(1, 4):
            total = total + dot(activ[r, spot[k]], cot[r][...], 0, 0)
        scaled = (total * scale).astype(BF)
        if k == 3:
            for h in range(2):
                rows = slice(128 * h, 128 * h + 128)
                grad_scale = grad_scale + jnp.sum(
                    total[rows] * far[h][0:128, :].astype(F32), axis=0, keepdims=True
                )
                far_grads[h][...] = scaled[rows]
        else:
            grad_scale = grad_scale + jnp.sum(total * wout[k][...].astype(F32), axis=0, keepdims=True)
            grads[k][...] = scaled
    extras[1:2, :] = grad_scale


def outer(spot, activ, cot, wout, far, table):
    out = call(
        outer_body,
        11,
        [((256, 1024), BF)] * 3 + [((128, 1024), BF)] * 2 + [((2, 1024), F32)],
        limit=8,
        micros=6,
    )(spot, activ, *cot, *wout, *far, table)
    return out[0:3], out[3:5], out[5]


def mix_body(spot, up, down, first, second, to_up, to_down):
    to_up[0:128, :] = (up[0:128, :].astype(F32) + first[...].astype(F32)).astype(BF)
    to_up[128:256, :] = up[128:256, :]
    to_down[0:128, :] = down[0:128, :]
    to_down[128:256, :] = (down[128:256, :].astype(F32) + second[...].astype(F32)).astype(BF)


def mix(spot, up, down, first, second):
    return call(mix_body, 4, [((256, 1024), BF)] * 2)(spot, up, down, first, second)


def mix_piped(spot, up, down, first, second):
    return piped(mix_body, [((256, 1024), BF)] * 2, limit=6)(spot, up, down, first, second)


def back_body(spot, *refs):
    cot = refs[0:4]
    slope = refs[4]
    win = refs[5:8] + (refs[18],)
    wout = refs[8:11] + (refs[19],)
    far = refs[11:13]
    table = refs[13]
    pre_low = refs[14]
    home = refs[15]
    away = refs[16]
    bias = refs[17]
    low = refs[20]
    for h in range(2):
        wout[3][128 * h : 128 * h + 128, :] = far[h][0:128, :]
        win[3][128 * h : 128 * h + 128, :] = far[h][128:256, :]
    scale = table[53:54, :]
    for r in range(4):
        low[r] = (cot[r][...].astype(F32) * scale).astype(BF)
    for k in range(4):
        total = jnp.zeros((1, 256), F32)
        for r in range(4):
            grad = dot(low[r], wout[k][...], 1, 1) * slope[r, spot[k]].astype(F32)
            total = total + jnp.sum(grad, axis=0, keepdims=True)
            pre_low[r, spot[k]] = grad.astype(BF)
        bias[spot[k]] = total
    for k in range(4):
        for r in range(4):
            grad = dot(pre_low[r, 0], win[k][0:256, 0:256], 1, 1)
            for block in range(1, 4):
                grad = grad + dot(pre_low[r, block], win[k][0:256, 256 * block : 256 * block + 256], 1, 1)
            if r % 2:
                away[r // 2, spot[k]] = grad.astype(BF)
            else:
                home[r // 2, spot[k]] = grad.astype(BF)


def back(spot, cot, slope, win, wout, far, table):
    return call(
        back_body,
        14,
        [((4, 4, 392, 256), BF), ((2, 4, 392, 256), BF), ((2, 4, 392, 256), BF), ((4, 1, 256), F32)],
        [pltpu.VMEM((256, 1024), BF), pltpu.VMEM((256, 1024), BF), pltpu.VMEM((4, 392, 1024), BF)],
        limit=12,
        micros=10,
    )(spot, *cot, slope, *win, *wout, *far, table)


def weight_body(spot, *refs):
    normal = refs[0:2]
    pre_low = refs[2]
    grads = refs[3:6]
    far_grads = refs[6:8]
    for k in (3, 1, 2, 0):
        for block in range(4):
            cols = slice(256 * block, 256 * block + 256)
            total = dot(normal[0][0, spot[k]], pre_low[0, block], 0, 0)
            for r in range(1, 4):
                total = total + dot(normal[r % 2][r // 2, spot[k]], pre_low[r, block], 0, 0)
            if k == 3:
                for h in range(2):
                    far_grads[h][:, cols] = total[128 * h : 128 * h + 128].astype(BF)
            else:
                grads[k][:, cols] = total.astype(BF)


def weight(spot, normal, pre_low):
    out = call(
        weight_body,
        3,
        [((256, 1024), BF)] * 3 + [((128, 1024), BF)] * 2,
        limit=6,
        micros=20,
    )(spot, *normal, pre_low)
    return out[0:3], out[3:5]


def channel_body(spot, images, images_z, home, by_core, normed, inverse, table, bias, extras, *refs):
    total, out, wide, grid = refs
    gain_sum = [jnp.zeros((1, 256), F32) for _ in range(4)]
    shift_sum = [jnp.zeros((1, 256), F32) for _ in range(4)]
    dw_sum = [jnp.zeros((1, 256), F32) for _ in range(4)]
    for part, pixels in enumerate((images, images_z)):
        wide[part] = pixels[...].astype(F32)
        for start, size in spans(392):
            rows = slice(start, start + size)
            grads = []
            mean = jnp.zeros((size, 1), F32)
            cross = jnp.zeros((size, 1), F32)
            for block in range(4):
                cols = slice(256 * block, 256 * block + 256)
                grad = home[part, block, rows, :].astype(F32) + by_core[part, block, rows, :].astype(F32)
                unit = normed[part, block, rows, :].astype(F32)
                gain_sum[block] += jnp.sum(grad * unit, axis=0, keepdims=True)
                shift_sum[block] += jnp.sum(grad, axis=0, keepdims=True)
                scaled = grad * table[50:51, cols]
                mean += jnp.sum(scaled, axis=1, keepdims=True)
                cross += jnp.sum(scaled * unit, axis=1, keepdims=True)
                grads.append(scaled)
            mean = mean * (1.0 / 1024.0)
            cross = cross * (1.0 / 1024.0)
            factor = inverse[part, rows, 0:1]
            for block in range(4):
                cols = slice(256 * block, 256 * block + 256)
                value = factor * (grads[block] - mean - normed[part, block, rows, :].astype(F32) * cross)
                dw_sum[block] += jnp.sum(value, axis=0, keepdims=True)
                grid[part, rows, cols] = value
    for block in range(4):
        cols = slice(256 * block, 256 * block + 256)
        out[block, 49:50, :] = dw_sum[block]
        out[block, 50:51, :] = gain_sum[block]
        out[block, 51:52, :] = shift_sum[block]
        out[block, 52:54, :] = extras[:, cols]
        out[block, 54:55, :] = bias[block]
        out[block, 55:56, :] = jnp.zeros((1, 256), F32)

    def lanes_step(block, carry):
        lanes = pl.ds(pl.multiple_of(block * 128, 128), 128)
        to_lanes = pl.ds(pl.multiple_of((block % 2) * 128, 128), 128)
        for r in range(7):
            acc = [jnp.zeros((8, 128), F32) for _ in range(7)]
            for part in range(2):
                for i in range(7):
                    row = i + r - 3
                    if row < 0 or row > 6:
                        continue
                    line = [wide[part, 8 * (7 * row + j) : 8 * (7 * row + j) + 8, lanes] for j in range(7)]
                    grads = [grid[part, 8 * (7 * i + j) : 8 * (7 * i + j) + 8, lanes] for j in range(7)]
                    for q in range(7):
                        for j in range(7):
                            if 0 <= j + q - 3 <= 6:
                                acc[q] = acc[q] + line[j + q - 3] * grads[j]
            for q in range(7):
                out[block // 2, 7 * r + q : 7 * r + q + 1, to_lanes] = jnp.sum(acc[q], axis=0, keepdims=True)
        return carry

    lax.fori_loop(0, 8, lanes_step, 0)
    for turn in range(4):
        total[turn] = out[spot[8 + turn]]


def channel(spot, *operands):
    return piped(
        channel_body,
        [((4, 56, 256), F32)],
        [pltpu.VMEM((4, 56, 256), F32), pltpu.VMEM((2, 392, 1024), F32), pltpu.VMEM((2, 392, 1024), F32)],
        limit=56,
        micros=2,
    )(spot, *operands)


def rows_body(spot, own, from_down, from_up, base_own, base_depth, base_both, *outs):
    bases = (base_own, base_both.at[0:64], base_depth.at[0:64], base_both.at[64:128])
    for r in range(4):
        rows = pl.ds(pl.multiple_of(64 * spot[4 + r], 64), 64)
        to = slice(64 * (r % 2), 64 * (r % 2) + 64)
        total = own[rows, :].astype(F32) + from_down[rows, :].astype(F32) + from_up[rows, :].astype(F32)
        outs[r // 2][to, :] = total.astype(BF)
        outs[2 + r // 2][to, :] = (bases[r][...].astype(F32) - LEARN_RATE * total).astype(BF)


def rows_of(spot, *operands):
    return call(rows_body, 6, [((128, 1024), BF)] * 4, limit=8)(spot, *operands)


def shift_body(spot, own, from_down, from_up, param, moment, new_moment, stepped, low):
    for start in range(0, 256, 64):
        rows = slice(start, start + 64)
        grad = own[rows, :].astype(F32) + from_down[rows, :].astype(F32) + from_up[rows, :].astype(F32)
        fresh = MOMENTUM_BETA * moment[rows, :] + grad
        moved = param[rows, :] - LEARN_RATE * fresh
        new_moment[rows, :] = fresh
        stepped[rows, :] = moved
        low[rows, :] = moved.astype(BF)


def shift(spot, *operands):
    return call(
        shift_body, 5, [((256, 1024), F32), ((256, 1024), F32), ((256, 1024), BF)], limit=8, micros=20
    )(spot, *operands)


def step_body(spot, *refs):
    here, by_depth, peer_here, peer_depth, by_core = refs[0:5]
    pieces = (here.at[0:64], by_core.at[0:64], by_depth.at[0:64], by_core.at[64:128])
    peers = (peer_here.at[0:64], by_core.at[128:192], peer_depth.at[0:64], by_core.at[192:256])
    param, moment, new_param, new_moment = refs[5:]
    for r in range(4):
        for block in range(4):
            lanes = pl.ds(pl.multiple_of((4 * block + spot[4 + r]) * 256, 256), 256)
            cols = slice(256 * block, 256 * block + 256)
            fresh = MOMENTUM_BETA * moment[:, lanes] + pieces[r][:, cols].astype(F32)
            after_step = param[:, lanes] - LEARN_RATE * fresh
            new_moment[:, lanes] = fresh
            new_param[:, lanes] = 0.5 * (after_step + peers[r][:, cols].astype(F32))


def step(spot, *operands):
    return call(step_body, 7, [((64, 4096), F32), ((64, 4096), F32)], limit=8)(spot, *operands)


def run(
    images,
    cotangent,
    weight_in,
    weight_out,
    channel_table,
    bias_in,
    moment_in,
):
    place = lax.axis_index("shard")
    x = place // 4
    t = place % 4
    spot = jnp.stack([x, (x + 1) % 4, (x + 3) % 4, (x + 2) % 4, t, t ^ 1, t ^ 2, t ^ 3, x, x ^ 1, x ^ 2, x ^ 3]).astype(jnp.int32)
    grid_images = images[0].transpose(1, 2, 0, 3).reshape(392, 1024)
    grid_cot = cotangent[0].transpose(1, 2, 0, 3).reshape(392, 1024)

    images_z = move(grid_images, DEPTH)
    cot_z = move(after(grid_cot, images_z), DEPTH)

    table_own = channel_table[0].T
    cut_own, cut_core, cut_away, wout_own = cut(spot, weight_in[0], weight_out[0], table_own)
    cut_depth = move(cut_away, DEPTH)
    wout_down = move(wout_own, X_UP)
    wout_up = move(wout_own, X_DOWN)
    cut_both = move(jnp.concatenate([cut_core, cut_depth[80:160]], axis=0), CORE)
    joined = join(spot, cut_own, cut_depth, after(cut_both, wout_down, wout_up), bias_in)
    joined_down = move(joined, X_UP)
    joined_up = move(joined, X_DOWN)
    tail_far = move(joined[256:272], X_FAR)
    packs = (joined[256:272], joined_up[256:272], joined_down[256:272], tail_far)
    far = (
        move(jnp.concatenate([wout_down[0:128], joined_down[0:128]], axis=0), X_UP),
        move(jnp.concatenate([wout_up[128:256], joined_up[128:256]], axis=0), X_DOWN),
    )
    win = (joined, joined_up, joined_down)
    wout = (wout_own, wout_up, wout_down)

    normal_own, normed, inverse, table = norm(spot, grid_images, images_z, packs)
    base_own, base_core, base_away = ahead(spot, weight_in[0], moment_in[0])
    base_depth = move(after(base_away, cot_z), DEPTH)
    normal = (normal_own, move(after(normal_own, *far, cot_z), CORE))
    activ, slope = forward(spot, normal, win, far, table)
    base_core, base_far, _ = lax.optimization_barrier((base_core, base_depth, slope))
    base_both = move(jnp.concatenate([base_core, base_far[64:128]], axis=0), CORE)
    cot = (grid_cot, move(after(grid_cot, images_z), CORE), cot_z, move(after(cot_z, normal_own), CORE))
    out_near, out_far, extras = outer(spot, activ, cot, wout, far, table)
    out_first = move(out_far[0], X_UP)
    out_second = move(out_far[1], X_DOWN)
    pre_low, home, away, grad_bias = back(spot, cot, after(slope, extras, base_both), win, wout, far, table)
    by_core = move(away, CORE)
    out_up, out_down = mix(spot, after(out_near[1], home), out_near[2], out_first, out_second)
    in_near, in_far = weight(spot, normal, after(pre_low, out_up))

    out_from_down = move(out_up, X_UP)
    out_from_up = move(out_down, X_DOWN)

    (small,) = channel(
        spot,
        grid_images,
        images_z,
        after(home, out_up),
        by_core,
        normed,
        inverse,
        table,
        grad_bias,
        extras,
    )
    in_up, in_down = mix_piped(
        spot, after(in_near[1], small), in_near[2], move(in_far[0], X_UP), move(in_far[1], X_DOWN)
    )
    return (
        (spot, in_near[0], in_up, in_down, small, out_near[0], out_from_down, out_from_up)
        + (base_own, base_depth, base_both)
    )


def finish(
    level,
    spot,
    in_own,
    in_up,
    in_down,
    small,
    out_own,
    out_from_down,
    out_from_up,
    base_own,
    base_depth,
    base_both,
    weight_in,
    weight_out,
    channel_table,
    bias_in,
    moment_in,
    moment_out,
    moment_table,
    moment_bias,
):
    mask = 2**level
    swap = [(g, g ^ mask) for g in range(8)]

    def partner(value, turn):
        route = [
            (16 * g + 4 * x_at + t_at, 16 * (g ^ mask) + 4 * x_at + (t_at ^ turn))
            for g in range(8)
            for x_at, t_at in SPOTS
        ]
        return lax.ppermute(value, ("gossip", "shard"), route)

    def average(own, low):
        return 0.5 * (own + lax.ppermute(low, "gossip", swap).astype(F32))

    in_from_down = move(in_up, X_UP)
    in_from_up = move(in_down, X_DOWN)
    new_moment_out, stepped_out, low_out = shift(
        spot, out_own, out_from_down, out_from_up, weight_out[0], moment_out[0]
    )
    new_out = average(stepped_out, low_out)
    here, away, peer_here, peer_away = rows_of(
        spot, after(in_own, low_out), in_from_down, in_from_up, base_own, base_depth, base_both
    )
    by_depth = move(away, DEPTH)
    from_here = partner(peer_here, 0)
    from_depth = partner(peer_away, 2)
    across = move(
        jnp.concatenate(
            [here[64:128], after(by_depth, new_out)[64:128], from_here[64:128], from_depth[64:128]], axis=0
        ),
        CORE,
    )
    new_in, new_moment_in = step(
        spot, here, by_depth, from_here, from_depth, across, weight_in[0], moment_in[0]
    )

    t = spot[4]
    by_t = in_order(t, [small[:, :54, 64 * a : 64 * a + 64] for a in range(4)])
    half_t = jnp.stack(by_t[0:2]) + move(jnp.stack(by_t[2:4]).astype(BF), DEPTH).astype(F32)
    full_t = half_t[0] + move(half_t[1].astype(BF), CORE).astype(F32)
    both = jnp.concatenate([full_t, small[:, 54].reshape(4, 4, 64)], axis=1)
    half_x = both[0:2] + move(both[2:4].astype(BF), X_FAR).astype(F32)
    total = half_x[0] + move(half_x[1].astype(BF), X_NEXT).astype(F32)
    total_table = total[:54]
    total_bias = total[54:].reshape(1, 256)

    def update(param, moment, grad):
        fresh = MOMENTUM_BETA * moment + grad
        return fresh, param - LEARN_RATE * fresh

    new_moment_table, stepped_table = update(channel_table[0].T, moment_table[0].T, total_table)
    new_moment_bias, stepped_bias = update(bias_in, moment_bias, total_bias)
    stepped_small = jnp.concatenate([stepped_table, stepped_bias.reshape(4, 64)], axis=0)
    new_small = average(stepped_small, stepped_small.astype(BF))
    return (
        new_in[None],
        new_out[None],
        new_small[:54].T[None],
        new_small[54:].reshape(1, 256),
        new_moment_in[None],
        new_moment_out[None],
        new_moment_table.T[None],
        new_moment_bias,
    )


def on_device(*args):
    levels = lax.axis_size("gossip").bit_length() - 1
    middle = run(*args[:7])
    branches = [partial(finish, level) for level in range(levels)]
    return lax.switch(args[-1][0] % levels, branches, *middle, *args[2:10])


def solution(mesh):
    in_specs = (
        P("gossip", "shard", None, None, None),
        P("gossip", "shard", None, None, None),
        P("gossip", "shard", None),
        P("gossip", "shard", None),
        P("gossip", "shard", None),
        P("gossip", "shard"),
        P("gossip", "shard", None),
        P("gossip", "shard", None),
        P("gossip", "shard", None),
        P("gossip", "shard"),
        P(),
    )
    out_specs = (
        P("gossip", "shard", None),
        P("gossip", "shard", None),
        P("gossip", "shard", None),
        P("gossip", "shard"),
        P("gossip", "shard", None),
        P("gossip", "shard", None),
        P("gossip", "shard", None),
        P("gossip", "shard"),
    )
    return jax.shard_map(
        on_device, mesh=mesh, in_specs=in_specs, out_specs=out_specs, check_vma=False
    )
```
